128 devices in a mesh: outer: 4 (over y_hi, core), blk: 32 (over z, y_lo, x).
Axes of the slice: x: 4, y: 4 (y_hi: 2, y_lo: 2; y = y_hi * 2 + y_lo), z: 4, core: 2. Of those that a mesh axis runs over, the one named last changes fastest.
Arguments:
- image_tower: bfloat16 [131072, 1152], P(('outer', 'blk')), may hold values from -20 to 20
- text_tower: bfloat16 [131072, 1152], P(('outer', 'blk')), may hold values from -20 to 20
- log_scale: float32 [1], replicated, may hold values from 2 to 2.5
- bias: float32 [1], replicated, may hold values from -9 to -7
Outputs:
- loss: float32 [1], replicated
- image_grad: float32 [131072, 1152], P(('outer', 'blk'))
- text_grad: float32 [131072, 1152], P(('outer', 'blk'))
- scalar_grads: float32 [2], replicated
The draws below stay inside these ranges and needn't reach their ends.
All inputs are finite; a program needn't handle non-finite values.
Results may differ from the reference program's by a relative error of at most 0.003.
Values may be sent and summed in bfloat16 or wider, within the bound.
No kernel may reach another device: no remote copies, remote signals or barrier semaphores. Data moves between devices by JAX's collectives and lax.ppermute only.
A program may use at most 128 MiB of HBM per device.

```python
import jax
import jax.numpy as jnp
from jax import lax

D = 1152
IMG_DEV = 1024
STEPS = 2
PAIRS = 131072
N_OUTER = 4
N_BLK = 32


def shared_latents(key):
    topic_count = 32
    common = jnp.clip(jax.random.normal(jax.random.fold_in(key, 11), (D,), jnp.float32), -4.0, 4.0)
    paired = jnp.clip(jax.random.normal(jax.random.fold_in(key, 12), (PAIRS, D), jnp.float32), -4.0, 4.0)
    topic_table = jnp.clip(jax.random.normal(jax.random.fold_in(key, 14), (topic_count, D), jnp.float32), -3.0, 3.0)
    topic_of = jax.random.randint(jax.random.fold_in(key, 15), (PAIRS,), 0, topic_count)
    topical = topic_table[topic_of]
    rising = 1.0 + jnp.arange(PAIRS, dtype=jnp.float32) / PAIRS
    return common[None, :] + 2.0 * topical + rising[:, None] * paired


def tower_noise(key):
    base = shared_latents(key)
    return base


def draw_image_tower(key, part):
    base = tower_noise(key)
    key = jax.random.fold_in(key, 1)
    noise_part = jnp.clip(jax.random.normal(key, (PAIRS, D), jnp.float32), -4.0, 4.0)
    return ((base + noise_part) * 0.1).astype(jnp.bfloat16)


def draw_text_tower(key, part):
    base = tower_noise(key)
    key = jax.random.fold_in(key, 2)
    noise_part = jnp.clip(jax.random.normal(key, (PAIRS, D), jnp.float32), -4.0, 4.0)
    return ((base + noise_part) * 0.1).astype(jnp.bfloat16)


def setup_inputs(seed: int = 0) -> dict:
    key_list = jax.random.split(jax.random.key(seed), 5)
    return {
        "image_tower": draw_image_tower(jax.random.fold_in(key_list[4], 71), 0),
        "text_tower": draw_text_tower(jax.random.fold_in(key_list[4], 71), 0),
        "log_scale": jnp.clip(jax.random.uniform(key_list[2], (1,), jnp.float32, 2.0, 2.5), 2.0, 2.5),
        "bias": jnp.clip(jax.random.uniform(key_list[3], (1,), jnp.float32, -9.0, -7.0), -9.0, -7.0),
    }


def normalize(tower):
    widened = tower.astype(jnp.float32)
    inverse = lax.rsqrt(lax.optimization_barrier(jnp.sum(widened * widened, axis=-1, keepdims=True)) + 1e-06)
    exact = widened * inverse
    return (exact.astype(jnp.bfloat16), exact, inverse)

def unit_backward(exact, inverse, dunit):
    return (dunit - exact * lax.optimization_barrier(jnp.sum(exact * dunit, axis=-1, keepdims=True))) * inverse

def score_tile(img_unit, txt_unit, logit_scale, logit_bias, positive):
    cosine = lax.dot_general(img_unit, txt_unit, (((1,), (1,)), ((), ())), preferred_element_type=jnp.float32)
    logit = logit_scale * cosine + logit_bias
    loss_sum = jnp.sum(jax.nn.softplus(logit))
    pair_grad = jax.nn.sigmoid(logit)
    if positive:
        count = cosine.shape[0]
        diagonal_ones = (lax.broadcasted_iota(jnp.int32, (count, count), 0) == lax.broadcasted_iota(jnp.int32, (count, count), 1)).astype(jnp.float32)
        loss_sum = loss_sum - jnp.sum(diagonal_ones * logit)
        pair_grad = pair_grad - diagonal_ones
    grad_low = pair_grad.astype(jnp.bfloat16)
    img_dunit = logit_scale * jnp.dot(grad_low, txt_unit, preferred_element_type=jnp.float32)
    txt_dunit = logit_scale * lax.dot_general(grad_low, img_unit, (((0,), (0,)), ((), ())), preferred_element_type=jnp.float32)
    return (loss_sum, img_dunit, txt_dunit, jnp.sum(pair_grad * cosine), jnp.sum(pair_grad))

def reference(image_tower, text_tower, log_scale, bias):
    img_unit, img_exact, img_inverse = normalize(image_tower)
    txt_unit, txt_exact, txt_inverse = normalize(text_tower)
    logit_scale = jnp.exp(log_scale[0])
    logit_bias = bias[0]
    grid_shape = (N_OUTER, N_BLK, IMG_DEV, D)
    img_blocks = img_unit.reshape(grid_shape)
    txt_blocks = txt_unit.reshape(grid_shape)
    img_dunit = jnp.zeros(grid_shape, jnp.float32)
    txt_dunit = jnp.zeros(grid_shape, jnp.float32)
    loss_sum = jnp.zeros((), jnp.float32)
    cos_sum = jnp.zeros((), jnp.float32)
    grad_sum = jnp.zeros((), jnp.float32)
    for offset in range(STEPS + 1):
        others = jnp.roll(txt_blocks, offset, axis=1)

        def score_pair(pair, positive=offset == 0):
            return score_tile(pair[0], pair[1], logit_scale, logit_bias, positive)
        results = lax.map(score_pair, (img_blocks.reshape(-1, IMG_DEV, D), others.reshape(-1, IMG_DEV, D)))
        loss_sum = loss_sum + jnp.sum(results[0])
        img_dunit = img_dunit + results[1].reshape(grid_shape)
        txt_dunit = txt_dunit + jnp.roll(results[2].reshape(grid_shape), -offset, axis=1)
        cos_sum = cos_sum + jnp.sum(results[3])
        grad_sum = grad_sum + jnp.sum(results[4])
    image_grad = unit_backward(img_exact, img_inverse, img_dunit.reshape(PAIRS, D))
    text_grad = unit_backward(txt_exact, txt_inverse, txt_dunit.reshape(PAIRS, D))
    loss = (loss_sum / PAIRS).reshape(1)
    scalar_grads = jnp.stack([logit_scale * cos_sum, grad_sum]) / PAIRS
    return (loss, image_grad, text_grad, scalar_grads)
```

```python
import functools

import jax
import jax.numpy as jnp
from jax import lax
from jax.experimental import pallas as pl
from jax.experimental.pallas import tpu as pltpu
from jax.sharding import PartitionSpec as P

F32 = jnp.float32
BF16 = jnp.bfloat16
TILE = 256
CHUNKS = (384, 384, 256)
SMEM = pl.BlockSpec(memory_space=pltpu.SMEM)
VMEM = pl.BlockSpec(memory_space=pltpu.VMEM)
VMEM_LIMIT = 48 * 1024 * 1024


def passed_along(value, axis, steps):
    count = lax.axis_size(axis)
    pairs = [(source, (source + steps) % count) for source in range(count)]
    return lax.ppermute(value, axis, pairs)


def exact_of(tower):
    widened = tower.astype(F32)
    inverse = lax.rsqrt(jnp.sum(widened * widened, axis=-1, keepdims=True) + 1e-06)
    return widened * inverse, inverse


def unit_of(tower):
    return exact_of(tower)[0].astype(BF16)


def products(rows, others):
    return lax.dot_general(rows, others, (((1,), (1,)), ((), ())), preferred_element_type=F32)


def folded(values):
    return jnp.sum(values.reshape(values.shape[0] // 8, 8, values.shape[1]), axis=0)


def add_sums(sums, logit, exped, cosine, pair_grad):
    del logit
    sums[0] += folded(jnp.log1p(exped))
    sums[1] += folded(pair_grad * cosine)
    sums[2] += folded(pair_grad)


def scored(rows, others, scale, bias):
    cosine = products(rows, others)
    logit = scale * cosine + bias
    exped = jnp.exp(logit)
    return cosine, logit, exped, exped / (1.0 + exped)


def own_kernel(scal, image, text, image_unit, text_unit, image_dunit, text_dunit, totals, sums, grads):
    scale, bias = scal[0], scal[1]
    count = image.shape[0]
    sums[...] = jnp.zeros_like(sums)

    @pl.loop(0, count // TILE)
    def _(t):
        rows = pl.ds(pl.multiple_of(t * TILE, TILE), TILE)
        image_unit[rows, :] = unit_of(image[rows, :])
        text_unit[rows, :] = unit_of(text[rows, :])

    @pl.loop(0, count // TILE)
    def _(t):
        start = pl.multiple_of(t * TILE, TILE)
        rows = pl.ds(start, TILE)
        cosine, logit, exped, pair_grad = scored(image_unit[rows, :], text_unit[...], scale, bias)
        diagonal = (
            lax.broadcasted_iota(jnp.int32, cosine.shape, 0) + start
            == lax.broadcasted_iota(jnp.int32, cosine.shape, 1)
        )
        pair_grad = jnp.where(diagonal, pair_grad - 1.0, pair_grad)
        sums[0] += folded(jnp.log1p(exped) - jnp.where(diagonal, logit, 0.0))
        sums[1] += folded(pair_grad * cosine)
        sums[2] += folded(pair_grad)
        grad_low = pair_grad.astype(BF16)
        grads[rows, :] = grad_low
        image_dunit[rows, :] = scale * jnp.dot(grad_low, text_unit[...], preferred_element_type=F32)

    @pl.loop(0, count // TILE)
    def _(t):
        rows = pl.ds(pl.multiple_of(t * TILE, TILE), TILE)
        text_dunit[rows, :] = scale * lax.dot_general(
            grads[:, rows], image_unit[...], (((0,), (0,)), ((), ())), preferred_element_type=F32
        )

    for kind in range(3):
        totals[kind] = jnp.sum(sums[kind])


def own_block(scal, image, text):
    count, width = image.shape
    tower = jax.ShapeDtypeStruct((count, width), BF16)
    dunit = jax.ShapeDtypeStruct((count, width), F32)
    return pl.pallas_call(
        own_kernel,
        out_shape=(tower, tower, dunit, dunit, jax.ShapeDtypeStruct((3,), F32)),
        in_specs=[SMEM, VMEM, VMEM],
        out_specs=(VMEM, VMEM, VMEM, VMEM, SMEM),
        scratch_shapes=[pltpu.VMEM((3, 8, count), F32), pltpu.VMEM((count, count), BF16)],
        compiler_params=pltpu.CompilerParams(vmem_limit_bytes=VMEM_LIMIT),
        cost_estimate=pl.CostEstimate(flops=20_000_000_000, bytes_accessed=20_000_000, transcendentals=3_000_000),
        name="own_block",
    )(scal, image, text)


def next_kernel(
    scal, image_unit, text_unit, image, text, image_in, text_in, totals_in,
    image_dunit, text_dunit, totals, other_image, other_text, sums,
):
    scale, bias = scal[0], scal[1]
    count = image.shape[0]
    sums[...] = jnp.zeros_like(sums)

    @pl.loop(0, count // TILE)
    def _(t):
        rows = pl.ds(pl.multiple_of(t * TILE, TILE), TILE)
        other_image[rows, :] = unit_of(image[rows, :])
        other_text[rows, :] = unit_of(text[rows, :])

    @pl.loop(0, count // TILE)
    def _(t):
        rows = pl.ds(pl.multiple_of(t * TILE, TILE), TILE)
        cosine, logit, exped, pair_grad = scored(image_unit[rows, :], other_text[...], scale, bias)
        add_sums(sums, logit, exped, cosine, pair_grad)
        image_dunit[rows, :] = image_in[rows, :] + scale * jnp.dot(
            pair_grad.astype(BF16), other_text[...], preferred_element_type=F32
        )

    @pl.loop(0, count // TILE)
    def _(t):
        rows = pl.ds(pl.multiple_of(t * TILE, TILE), TILE)
        pair_grad = scored(text_unit[rows, :], other_image[...], scale, bias)[3]
        text_dunit[rows, :] = text_in[rows, :] + scale * jnp.dot(
            pair_grad.astype(BF16), other_image[...], preferred_element_type=F32
        )

    @pl.loop(0, count // TILE)
    def _(t):
        rows = pl.ds(pl.multiple_of(t * TILE, TILE), TILE)
        cosine, logit, exped, pair_grad = scored(other_image[rows, :], other_text[...], scale, bias)
        add_sums(sums, logit, exped, cosine, pair_grad)

    for kind in range(3):
        totals[kind] = totals_in[kind] + jnp.sum(sums[kind])


def next_block(scal, image_unit, text_unit, image, text, image_dunit, text_dunit, totals):
    count, width = image.shape
    dunit = jax.ShapeDtypeStruct((count, width), F32)
    return pl.pallas_call(
        next_kernel,
        out_shape=(dunit, dunit, jax.ShapeDtypeStruct((3,), F32)),
        in_specs=[SMEM] + [VMEM] * 6 + [SMEM],
        out_specs=(VMEM, VMEM, SMEM),
        scratch_shapes=[
            pltpu.VMEM((count, width), BF16),
            pltpu.VMEM((count, width), BF16),
            pltpu.VMEM((3, 8, count), F32),
        ],
        input_output_aliases={5: 0, 6: 1},
        compiler_params=pltpu.CompilerParams(vmem_limit_bytes=VMEM_LIMIT),
        cost_estimate=pl.CostEstimate(flops=30_000_000_000, bytes_accessed=30_000_000, transcendentals=6_000_000),
        name="next_block",
    )(scal, image_unit, text_unit, image, text, image_dunit, text_dunit, totals)


def chunk_kernel(
    scal, image_unit, text_unit, image, text, image_in, text_in, image_dunit, text_dunit, other_image, other_text
):
    scale, bias = scal[0], scal[1]

    @pl.when(pl.program_id(0) == 0)
    def _():
        other_image[...] = unit_of(image[...])
        other_text[...] = unit_of(text[...])

    for own, other, given, out in (
        (image_unit, other_text, image_in, image_dunit),
        (text_unit, other_image, text_in, text_dunit),
    ):
        pair_grad = scored(own[...], other[...], scale, bias)[3]
        out[...] = given[...] + scale * jnp.dot(pair_grad.astype(BF16), other[...], preferred_element_type=F32)


def chunk_block(scal, image_unit, text_unit, image, text, image_dunit, text_dunit):
    count, width = image_unit.shape
    rows = image.shape[0]
    dunit = jax.ShapeDtypeStruct((count, width), F32)
    tile = pl.BlockSpec((TILE, width), lambda t: (t, 0))
    whole = pl.BlockSpec((rows, width), lambda t: (0, 0))
    return pl.pallas_call(
        chunk_kernel,
        grid=(count // TILE,),
        out_shape=(dunit, dunit),
        in_specs=[SMEM, tile, tile, whole, whole, tile, tile],
        out_specs=(tile, tile),
        scratch_shapes=[pltpu.VMEM((rows, width), BF16), pltpu.VMEM((rows, width), BF16)],
        input_output_aliases={5: 0, 6: 1},
        compiler_params=pltpu.CompilerParams(vmem_limit_bytes=VMEM_LIMIT),
        cost_estimate=pl.CostEstimate(
            flops=8 * count * rows * width, bytes_accessed=24_000_000, transcendentals=2 * count * rows
        ),
        name="chunk_block",
    )(scal, image_unit, text_unit, image, text, image_dunit, text_dunit)


def last_kernel(
    scal, image_own, text_own, image, text, image_in, text_in, image_grad, text_grad, other_image, other_text
):
    scale, bias = scal[0], scal[1]

    @pl.when(pl.program_id(0) == 0)
    def _():
        other_image[...] = unit_of(image[...])
        other_text[...] = unit_of(text[...])

    for own, other, given, out in (
        (image_own, other_text, image_in, image_grad),
        (text_own, other_image, text_in, text_grad),
    ):
        exact, inverse = exact_of(own[...])
        pair_grad = scored(exact.astype(BF16), other[...], scale, bias)[3]
        dunit = given[...] + scale * jnp.dot(pair_grad.astype(BF16), other[...], preferred_element_type=F32)
        out[...] = (dunit - exact * jnp.sum(exact * dunit, axis=-1, keepdims=True)) * inverse


def last_block(scal, image_own, text_own, image, text, image_dunit, text_dunit):
    count, width = image_own.shape
    rows = image.shape[0]
    grad = jax.ShapeDtypeStruct((count, width), F32)
    tile = pl.BlockSpec((TILE, width), lambda t: (t, 0))
    whole = pl.BlockSpec((rows, width), lambda t: (0, 0))
    return pl.pallas_call(
        last_kernel,
        grid=(count // TILE,),
        out_shape=(grad, grad),
        in_specs=[SMEM, tile, tile, whole, whole, tile, tile],
        out_specs=(tile, tile),
        scratch_shapes=[pltpu.VMEM((rows, width), BF16), pltpu.VMEM((rows, width), BF16)],
        compiler_params=pltpu.CompilerParams(vmem_limit_bytes=VMEM_LIMIT),
        cost_estimate=pl.CostEstimate(
            flops=8 * count * rows * width, bytes_accessed=24_000_000, transcendentals=2 * count * rows
        ),
        name="last_block",
    )(scal, image_own, text_own, image, text, image_dunit, text_dunit)


def per_device(image_tower, text_tower, log_scale, bias):
    scal = jnp.concatenate([jnp.exp(log_scale), bias])
    starts = [sum(CHUNKS[:i]) for i in range(len(CHUNKS))]
    pieces = [slice(s, s + c) for s, c in zip(starts, CHUNKS)]
    text_one = [passed_along(text_tower[p], "blk", 1) for p in pieces]
    image_one = [passed_along(image_tower[p], "blk", -1) for p in pieces]
    text_two = [passed_along(t, "blk", 1) for t in text_one]
    image_two = [passed_along(t, "blk", -1) for t in image_one]
    image_unit, text_unit, image_dunit, text_dunit, totals = own_block(scal, image_tower, text_tower)
    image_dunit, text_dunit, totals = next_block(
        scal, image_unit, text_unit, jnp.concatenate(image_one), jnp.concatenate(text_one),
        image_dunit, text_dunit, totals,
    )
    sums = lax.psum(totals, ("outer", "blk"))
    for text, image in zip(text_two[:-1], image_two[:-1]):
        image_dunit, text_dunit = chunk_block(scal, image_unit, text_unit, image, text, image_dunit, text_dunit)
    image_grad, text_grad = last_block(
        scal, image_tower, text_tower, image_two[-1], text_two[-1], image_dunit, text_dunit
    )
    pair_count = text_tower.shape[0] * lax.axis_size("outer") * lax.axis_size("blk")
    loss = sums[:1] / pair_count
    scalar_grads = jnp.stack([scal[0] * sums[1], sums[2]]) / pair_count
    return (loss, image_grad, text_grad, scalar_grads)


def solution(mesh):
    return jax.shard_map(
        per_device,
        mesh=mesh,
        in_specs=(P(("outer", "blk"), None), P(("outer", "blk"), None), P(), P()),
        out_specs=(P(), P(("outer", "blk"), None), P(("outer", "blk"), None), P()),
        check_vma=False,
    )
```

```python
import functools

import jax
import jax.numpy as jnp
from jax import lax
from jax.experimental import pallas as pl
from jax.experimental.pallas import tpu as pltpu
from jax.sharding import PartitionSpec as P

F32 = jnp.float32
BF16 = jnp.bfloat16
TILE = 256
LAST_TILE = 256
SPLIT = 768
SMEM = pl.BlockSpec(memory_space=pltpu.SMEM)
VMEM = pl.BlockSpec(memory_space=pltpu.VMEM)
VMEM_LIMIT = 24 * 1024 * 1024
LAST_LIMIT = 30 * 1024 * 1024
BOTH = ("outer", "blk")


def passed_along(value, axis, steps):
    count = lax.axis_size(axis)
    pairs = [(source, (source + steps) % count) for source in range(count)]
    return lax.ppermute(value, axis, pairs)


def summed(totals):
    for axis, bit in (("outer", 1), ("outer", 2), ("blk", 4), ("blk", 8), ("blk", 16), ("blk", 2), ("blk", 1)):
        pairs = [(source, source ^ bit) for source in range(lax.axis_size(axis))]
        totals = totals + lax.ppermute(totals, axis, pairs)
    return totals


def inverse_of(widened):
    return lax.rsqrt(jnp.sum(widened * widened, axis=-1, keepdims=True) + 1e-06)


def unit_of(tower):
    widened = tower.astype(F32)
    return (widened * inverse_of(widened)).astype(BF16)


def products(rows, others):
    return lax.dot_general(rows, others, (((1,), (1,)), ((), ())), preferred_element_type=F32)


def weighted(pair_grad, others):
    return jnp.dot(pair_grad.astype(BF16), others, preferred_element_type=F32)


def sigmoid_of(rows, others, scale, bias):
    return 1.0 / (1.0 + jnp.exp(-scale * products(rows, others) - bias))


def folded(values):
    return jnp.sum(values.reshape(values.shape[0] // 8, 8, values.shape[1]), axis=0)


def scored(sums, rows, others, scale, bias):
    cosine = products(rows, others)
    exped = jnp.exp(scale * cosine + bias)
    pair_grad = exped / (1.0 + exped)
    width = others.shape[0]
    sums[0, :, :width] += folded(jnp.log1p(exped))
    sums[1, :, :width] += folded(pair_grad * cosine)
    sums[2, :, :width] += folded(pair_grad)
    return pair_grad


def tile_at(step):
    return pl.ds(pl.multiple_of(step * TILE, TILE), TILE)


def own_kernel(scal, image, text, image_unit, text_unit, image_dunit, text_dunit, totals, sums, grads):
    scale, bias = scal[0], scal[1]
    steps = image.shape[0] // TILE
    sums[...] = jnp.zeros_like(sums)

    @pl.loop(0, steps)
    def _(t):
        rows = tile_at(t)
        image_unit[rows, :] = unit_of(image[rows, :])
        text_unit[rows, :] = unit_of(text[rows, :])

    @pl.loop(0, steps)
    def _(t):
        rows = tile_at(t)
        cosine = products(image_unit[rows, :], text_unit[...])
        logit = scale * cosine + bias
        exped = jnp.exp(logit)
        pair_grad = exped / (1.0 + exped)
        diagonal = (
            lax.broadcasted_iota(jnp.int32, cosine.shape, 0) + t * TILE
            == lax.broadcasted_iota(jnp.int32, cosine.shape, 1)
        )
        pair_grad = jnp.where(diagonal, pair_grad - 1.0, pair_grad)
        sums[0] += folded(jnp.log1p(exped) - jnp.where(diagonal, logit, 0.0))
        sums[1] += folded(pair_grad * cosine)
        sums[2] += folded(pair_grad)
        grads[rows, :] = pair_grad.astype(BF16)
        image_dunit[rows, :] = weighted(pair_grad, text_unit[...])

    @pl.loop(0, steps)
    def _(t):
        rows = tile_at(t)
        text_dunit[rows, :] = lax.dot_general(
            grads[:, rows], image_unit[...], (((0,), (0,)), ((), ())), preferred_element_type=F32
        )

    for kind in range(3):
        totals[kind] = jnp.sum(sums[kind])


def own_block(scal, image, text):
    count, width = image.shape
    tower = jax.ShapeDtypeStruct((count, width), BF16)
    dunit = jax.ShapeDtypeStruct((count, width), F32)
    return pl.pallas_call(
        own_kernel,
        out_shape=(tower, tower, dunit, dunit, jax.ShapeDtypeStruct((3,), F32)),
        in_specs=[SMEM, VMEM, VMEM],
        out_specs=(VMEM, VMEM, VMEM, VMEM, SMEM),
        scratch_shapes=[pltpu.VMEM((3, 8, count), F32), pltpu.VMEM((count, count), BF16)],
        compiler_params=pltpu.CompilerParams(vmem_limit_bytes=VMEM_LIMIT),
        cost_estimate=pl.CostEstimate(flops=3000000000, bytes_accessed=1_000_000, transcendentals=0),
        name="own_block",
    )(scal, image, text)


def tile_spec(width):
    return pl.BlockSpec((TILE, width), lambda t: (t, 0))


def whole_spec(piece):
    return pl.BlockSpec(piece.shape, lambda t: (0, 0), pipeline_mode=pl.Buffered(1))


def piece_kernel(
    scal, image_unit, text_unit, image, text, image_in, text_in, totals_in,
    image_dunit, text_dunit, totals, other_image, other_text, sums,
):
    scale, bias = scal[0], scal[1]

    @pl.when(pl.program_id(0) == 0)
    def _():
        other_image[...] = unit_of(image[...])
        other_text[...] = unit_of(text[...])
        sums[...] = jnp.zeros_like(sums)

    pair_grad = scored(sums, image_unit[...], other_text[...], scale, bias)
    image_dunit[...] = image_in[...] + weighted(pair_grad, other_text[...])
    pair_grad = sigmoid_of(text_unit[...], other_image[...], scale, bias)
    text_dunit[...] = text_in[...] + weighted(pair_grad, other_image[...])

    @pl.when(pl.program_id(0) == pl.num_programs(0) - 1)
    def _():
        for kind in range(3):
            totals[kind] = totals_in[kind] + jnp.sum(sums[kind])


def piece_block(scal, image_unit, text_unit, image, text, image_dunit, text_dunit, totals):
    count, width = image_unit.shape
    rows = image.shape[0]
    dunit = jax.ShapeDtypeStruct((count, width), F32)
    tile = tile_spec(width)
    return pl.pallas_call(
        piece_kernel,
        grid=(count // TILE,),
        out_shape=(dunit, dunit, jax.ShapeDtypeStruct((3,), F32)),
        in_specs=[SMEM, tile, tile, whole_spec(image), whole_spec(text), tile, tile, SMEM],
        out_specs=(tile, tile, SMEM),
        scratch_shapes=[pltpu.VMEM((rows, width), BF16), pltpu.VMEM((rows, width), BF16), pltpu.VMEM((3, 8, rows), F32)],
        input_output_aliases={5: 0, 6: 1},
        compiler_params=pltpu.CompilerParams(vmem_limit_bytes=VMEM_LIMIT),
        cost_estimate=pl.CostEstimate(flops=1000, bytes_accessed=1_000_000, transcendentals=0),
        name="piece_block",
    )(scal, image_unit, text_unit, image, text, image_dunit, text_dunit, totals)


def middle_kernel(
    scal, image_unit, text_unit, image_a, image_b, text_a, text_b, image_in, text_in, totals_in,
    image_dunit, text_dunit, totals, other_image, other_text, sums,
):
    scale, bias = scal[0], scal[1]
    step = pl.program_id(0)
    split = image_a.shape[0]

    @pl.when(step == 0)
    def _():
        other_image[:split, :] = unit_of(image_a[...])
        other_image[split:, :] = unit_of(image_b[...])
        other_text[:split, :] = unit_of(text_a[...])
        other_text[split:, :] = unit_of(text_b[...])
        sums[...] = jnp.zeros_like(sums)

    pair_grad = scored(sums, image_unit[...], other_text[split:, :], scale, bias)
    image_dunit[...] = image_in[...] + weighted(pair_grad, other_text[split:, :])
    pair_grad = sigmoid_of(text_unit[...], other_image[split:, :], scale, bias)
    text_dunit[...] = text_in[...] + weighted(pair_grad, other_image[split:, :])
    scored(sums, other_image[tile_at(step), :], other_text[...], scale, bias)

    @pl.when(step == pl.num_programs(0) - 1)
    def _():
        for kind in range(3):
            totals[kind] = totals_in[kind] + jnp.sum(sums[kind])


def middle_block(scal, image_unit, text_unit, image, text, image_dunit, text_dunit, totals):
    count, width = image_unit.shape
    dunit = jax.ShapeDtypeStruct((count, width), F32)
    tile = tile_spec(width)
    wholes = [whole_spec(piece) for piece in (*image, *text)]
    return pl.pallas_call(
        middle_kernel,
        grid=(count // TILE,),
        out_shape=(dunit, dunit, jax.ShapeDtypeStruct((3,), F32)),
        in_specs=[SMEM, tile, tile, *wholes, tile, tile, SMEM],
        out_specs=(tile, tile, SMEM),
        scratch_shapes=[
            pltpu.VMEM((count, width), BF16),
            pltpu.VMEM((count, width), BF16),
            pltpu.VMEM((3, 8, count), F32),
        ],
        input_output_aliases={7: 0, 8: 1},
        compiler_params=pltpu.CompilerParams(vmem_limit_bytes=VMEM_LIMIT),
        cost_estimate=pl.CostEstimate(flops=20000000000, bytes_accessed=1_000_000, transcendentals=0),
        name="middle_block",
    )(scal, image_unit, text_unit, *image, *text, image_dunit, text_dunit, totals)


def chunk_kernel(
    scal, image_unit, text_unit, image, text, image_in, text_in, image_dunit, text_dunit, other_image, other_text
):
    scale, bias = scal[0], scal[1]

    @pl.when(pl.program_id(0) == 0)
    def _():
        other_image[...] = unit_of(image[...])
        other_text[...] = unit_of(text[...])

    for own, other, given, out in (
        (image_unit, other_text, image_in, image_dunit),
        (text_unit, other_image, text_in, text_dunit),
    ):
        pair_grad = sigmoid_of(own[...], other[...], scale, bias)
        out[...] = given[...] + weighted(pair_grad, other[...])


def chunk_block(scal, image_unit, text_unit, image, text, image_dunit, text_dunit):
    count, width = image_unit.shape
    rows = image.shape[0]
    dunit = jax.ShapeDtypeStruct((count, width), F32)
    tile = tile_spec(width)
    return pl.pallas_call(
        chunk_kernel,
        grid=(count // TILE,),
        out_shape=(dunit, dunit),
        in_specs=[SMEM, tile, tile, whole_spec(image), whole_spec(text), tile, tile],
        out_specs=(tile, tile),
        scratch_shapes=[pltpu.VMEM((rows, width), BF16), pltpu.VMEM((rows, width), BF16)],
        input_output_aliases={5: 0, 6: 1},
        compiler_params=pltpu.CompilerParams(vmem_limit_bytes=VMEM_LIMIT),
        cost_estimate=pl.CostEstimate(flops=1000, bytes_accessed=1_000_000, transcendentals=0),
        name="chunk_block",
    )(scal, image_unit, text_unit, image, text, image_dunit, text_dunit)


def last_kernel(
    scal, image_own, text_own, image_unit, text_unit, image, text, image_in, text_in,
    image_grad, text_grad, other_image, other_text, image_out, text_out, sems,
):
    scale, bias = scal[0], scal[1]
    steps = image_own.shape[0] // LAST_TILE
    other_image[...] = unit_of(image[...])
    other_text[...] = unit_of(text[...])
    sides = (
        (image_own, image_unit, other_text, image_in, image_out, image_grad),
        (text_own, text_unit, other_image, text_in, text_out, text_grad),
    )
    copies = []
    for side, (own, unit, other, given, out, grad) in enumerate(sides):
        low = sigmoid_of(unit[...], other[...], scale, bias).astype(BF16)
        for step in range(steps):
            rows = slice(step * LAST_TILE, (step + 1) * LAST_TILE)
            dunit = given[rows, :] + jnp.dot(low[rows, :], other[...], preferred_element_type=F32)
            widened = own[rows, :].astype(F32)
            inverse = inverse_of(widened)
            along = jnp.sum(widened * dunit, axis=-1, keepdims=True) * inverse * inverse
            out[rows, :] = (dunit - widened * along) * (scale * inverse)
            copy = pltpu.make_async_copy(out.at[rows, :], grad.at[rows, :], sems.at[side, step])
            copy.start()
            copies.append(copy)
    for copy in copies:
        copy.wait()


def last_block(scal, image_own, text_own, image_unit, text_unit, image, text, image_dunit, text_dunit):
    count, width = image_own.shape
    rows = image.shape[0]
    grad = jax.ShapeDtypeStruct((count, width), F32)
    return pl.pallas_call(
        last_kernel,
        out_shape=(grad, grad),
        in_specs=[SMEM] + [VMEM] * 8,
        out_specs=(pl.BlockSpec(memory_space=pl.ANY), pl.BlockSpec(memory_space=pl.ANY)),
        scratch_shapes=[
            pltpu.VMEM((rows, width), BF16),
            pltpu.VMEM((rows, width), BF16),
            pltpu.VMEM((count, width), F32),
            pltpu.VMEM((count, width), F32),
            pltpu.SemaphoreType.DMA((2, count // LAST_TILE)),
        ],
        compiler_params=pltpu.CompilerParams(vmem_limit_bytes=LAST_LIMIT),
        cost_estimate=pl.CostEstimate(
            flops=8 * count * rows * width, bytes_accessed=24 * count * width, transcendentals=4 * count * rows
        ),
        name="last_block",
    )(scal, image_own, text_own, image_unit, text_unit, image, text, image_dunit, text_dunit)


def per_device(image_tower, text_tower, log_scale, bias):
    scal = jnp.concatenate([jnp.exp(log_scale), bias])
    text_a, text_b = (passed_along(p, "blk", 1) for p in (text_tower[:SPLIT], text_tower[SPLIT:]))
    image_a, image_b = (passed_along(p, "blk", -1) for p in (image_tower[:SPLIT], image_tower[SPLIT:]))
    image_unit, text_unit, image_dunit, text_dunit, totals = own_block(scal, image_tower, text_tower)
    image_a, text_a, image_dunit = lax.optimization_barrier((image_a, text_a, image_dunit))
    image_dunit, text_dunit, totals = piece_block(
        scal, image_unit, text_unit, image_a, text_a, image_dunit, text_dunit, totals
    )
    image_b, text_b, image_dunit = lax.optimization_barrier((image_b, text_b, image_dunit))
    far_text_a, far_text_b = (passed_along(p, "blk", 1) for p in (text_a, text_b))
    far_image_a, far_image_b = (passed_along(p, "blk", -1) for p in (image_a, image_b))
    image_dunit, text_dunit, totals = middle_block(
        scal, image_unit, text_unit, (image_a, image_b), (text_a, text_b), image_dunit, text_dunit, totals
    )
    sums = summed(totals)
    sums, scal = lax.optimization_barrier((sums, scal))
    image_dunit, text_dunit = chunk_block(
        scal, image_unit, text_unit, far_image_a, far_text_a, image_dunit, text_dunit
    )
    image_grad, text_grad = last_block(
        scal, image_tower, text_tower, image_unit, text_unit, far_image_b, far_text_b, image_dunit, text_dunit
    )
    pair_count = text_tower.shape[0] * lax.axis_size("outer") * lax.axis_size("blk")
    loss = sums[:1] / pair_count
    scalar_grads = jnp.stack([scal[0] * sums[1], sums[2]]) / pair_count
    return (loss, image_grad, text_grad, scalar_grads)


def solution(mesh):
    return jax.shard_map(
        per_device,
        mesh=mesh,
        in_specs=(P(BOTH, None), P(BOTH, None), P(), P()),
        out_specs=(P(), P(BOTH, None), P(BOTH, None), P()),
        check_vma=False,
    )
```

```python
import functools

import functools

import jax
import jax.numpy as jnp
from jax import lax
from jax.experimental import pallas as pl
from jax.experimental.pallas import tpu as pltpu
from jax.sharding import PartitionSpec as P

F32 = jnp.float32
BF16 = jnp.bfloat16
TILE = 256
LAST_TILE = 128
SPLIT = 512
PART = 256
OWN_FLOPS = 3_000_000_000
PIECE_FLOPS = 1_000
LOSS_FLOPS = 20_000_000_000
SIDE_FLOPS = 3_000_000_000
LAST_FLOPS = 3_000_000_000
EXCHANGES = (("outer", 1), ("outer", 2), ("blk", 4), ("blk", 8), ("blk", 16), ("blk", 2), ("blk", 1))
SMEM = pl.BlockSpec(memory_space=pltpu.SMEM)
VMEM = pl.BlockSpec(memory_space=pltpu.VMEM)
VMEM_LIMIT = 24 * 1024 * 1024
LAST_LIMIT = 30 * 1024 * 1024
BOTH = ("outer", "blk")


def passed_along(value, axis, steps):
    count = lax.axis_size(axis)
    pairs = [(source, (source + steps) % count) for source in range(count)]
    return lax.ppermute(value, axis, pairs)


def exchanged(totals, step):
    axis, bit = EXCHANGES[step]
    pairs = [(source, source ^ bit) for source in range(lax.axis_size(axis))]
    return totals + lax.ppermute(totals, axis, pairs)


def beside(totals, step, dunit, work):
    totals, dunit = lax.optimization_barrier((totals, dunit))
    return lax.optimization_barrier((exchanged(totals, step), work(dunit)))


def cost(flops):
    return pl.CostEstimate(flops=flops, bytes_accessed=1_000_000, transcendentals=0)


def inverse_of(widened):
    return lax.rsqrt(jnp.sum(widened * widened, axis=-1, keepdims=True) + 1e-06)


def unit_of(tower):
    widened = tower.astype(F32)
    return (widened * inverse_of(widened)).astype(BF16)


def products(rows, others):
    return lax.dot_general(rows, others, (((1,), (1,)), ((), ())), preferred_element_type=F32)


def weighted(pair_grad, others):
    return jnp.dot(pair_grad.astype(BF16), others, preferred_element_type=F32)


def sigmoid_of(rows, others, scale, bias):
    return pl.reciprocal(1.0 + jnp.exp(-scale * products(rows, others) - bias))


def folded(values):
    return jnp.sum(values.reshape(values.shape[0] // 8, 8, values.shape[1]), axis=0)


def scored(sums, rows, others, scale, bias):
    cosine = products(rows, others)
    exped = jnp.exp(scale * cosine + bias)
    above = 1.0 + exped
    inverse = pl.reciprocal(above)
    pair_grad = exped * inverse
    width = others.shape[0]
    sums[0, :, :width] += folded(jnp.log(above) + (exped - (above - 1.0)) * inverse)
    sums[1, :, :width] += folded(pair_grad * cosine)
    sums[2, :, :width] += folded(pair_grad)
    return pair_grad


def tile_at(step):
    return pl.ds(pl.multiple_of(step * TILE, TILE), TILE)


def own_kernel(scal, image, text, image_unit, text_unit, image_dunit, text_dunit, totals, sums, grads):
    scale, bias = scal[0], scal[1]
    steps = image.shape[0] // TILE
    sums[...] = jnp.zeros_like(sums)

    @pl.loop(0, steps)
    def _(t):
        rows = tile_at(t)
        image_unit[rows, :] = unit_of(image[rows, :])
        text_unit[rows, :] = unit_of(text[rows, :])

    @pl.loop(0, steps)
    def _(t):
        rows = tile_at(t)
        cosine = products(image_unit[rows, :], text_unit[...])
        logit = scale * cosine + bias
        exped = jnp.exp(logit)
        pair_grad = exped / (1.0 + exped)
        diagonal = (
            lax.broadcasted_iota(jnp.int32, cosine.shape, 0) + t * TILE
            == lax.broadcasted_iota(jnp.int32, cosine.shape, 1)
        )
        pair_grad = jnp.where(diagonal, pair_grad - 1.0, pair_grad)
        sums[0] += folded(jnp.log1p(exped) - jnp.where(diagonal, logit, 0.0))
        sums[1] += folded(pair_grad * cosine)
        sums[2] += folded(pair_grad)
        grads[rows, :] = pair_grad.astype(BF16)
        image_dunit[rows, :] = weighted(pair_grad, text_unit[...])

    @pl.loop(0, steps)
    def _(t):
        rows = tile_at(t)
        text_dunit[rows, :] = lax.dot_general(
            grads[:, rows], image_unit[...], (((0,), (0,)), ((), ())), preferred_element_type=F32
        )

    for kind in range(3):
        totals[kind] = jnp.sum(sums[kind])


def own_block(scal, image, text):
    count, width = image.shape
    tower = jax.ShapeDtypeStruct((count, width), BF16)
    dunit = jax.ShapeDtypeStruct((count, width), F32)
    return pl.pallas_call(
        own_kernel,
        out_shape=(tower, tower, dunit, dunit, jax.ShapeDtypeStruct((3,), F32)),
        in_specs=[SMEM, VMEM, VMEM],
        out_specs=(VMEM, VMEM, VMEM, VMEM, SMEM),
        scratch_shapes=[pltpu.VMEM((3, 8, count), F32), pltpu.VMEM((count, count), BF16)],
        compiler_params=pltpu.CompilerParams(vmem_limit_bytes=VMEM_LIMIT),
        cost_estimate=cost(OWN_FLOPS),
        name="own_block",
    )(scal, image, text)


def tiles(count):
    return [slice(start, start + TILE) for start in range(0, count, TILE)]


def piece_kernel(
    scal, image_unit, text_unit, image, text, image_in, text_in, totals_in,
    image_dunit, text_dunit, totals, other_image, other_text, sums,
):
    scale, bias = scal[0], scal[1]
    other_image[...] = unit_of(image[...])
    other_text[...] = unit_of(text[...])
    sums[...] = jnp.zeros_like(sums)
    for rows in tiles(image_unit.shape[0]):
        pair_grad = scored(sums, image_unit[rows, :], other_text[...], scale, bias)
        image_dunit[rows, :] = image_in[rows, :] + weighted(pair_grad, other_text[...])
        pair_grad = sigmoid_of(text_unit[rows, :], other_image[...], scale, bias)
        text_dunit[rows, :] = text_in[rows, :] + weighted(pair_grad, other_image[...])
    for rows in tiles(other_image.shape[0]):
        scored(sums, other_image[rows, :], other_text[...], scale, bias)
    for kind in range(3):
        totals[kind] = totals_in[kind] + jnp.sum(sums[kind])


def piece_block(scal, image_unit, text_unit, image, text, image_dunit, text_dunit, totals):
    count, width = image_unit.shape
    rows = image.shape[0]
    dunit = jax.ShapeDtypeStruct((count, width), F32)
    unit = jax.ShapeDtypeStruct((rows, width), BF16)
    return pl.pallas_call(
        piece_kernel,
        out_shape=(dunit, dunit, jax.ShapeDtypeStruct((3,), F32), unit, unit),
        in_specs=[SMEM] + [VMEM] * 6 + [SMEM],
        out_specs=(VMEM, VMEM, SMEM, VMEM, VMEM),
        scratch_shapes=[pltpu.VMEM((3, 8, rows), F32)],
        input_output_aliases={5: 0, 6: 1},
        compiler_params=pltpu.CompilerParams(vmem_limit_bytes=VMEM_LIMIT),
        cost_estimate=cost(PIECE_FLOPS),
        name="piece_block",
    )(scal, image_unit, text_unit, image, text, image_dunit, text_dunit, totals)


def loss_kernel(
    scal, image_unit, image, text, image_in, totals_in, image_before, text_before,
    image_dunit, totals, other_image, other_text, sums,
):
    scale, bias = scal[0], scal[1]
    other_image[...] = unit_of(image[...])
    other_text[...] = unit_of(text[...])
    sums[...] = jnp.zeros_like(sums)
    for rows in tiles(image_unit.shape[0]):
        pair_grad = scored(sums, image_unit[rows, :], other_text[...], scale, bias)
        image_dunit[rows, :] = image_in[rows, :] + weighted(pair_grad, other_text[...])
    for rows in tiles(other_image.shape[0]):
        for text_units in (other_text, text_before):
            scored(sums, other_image[rows, :], text_units[...], scale, bias)
    for rows in tiles(image_before.shape[0]):
        scored(sums, image_before[rows, :], other_text[...], scale, bias)
    for kind in range(3):
        totals[kind] = totals_in[kind] + jnp.sum(sums[kind])


def loss_block(scal, image_unit, image, text, image_dunit, totals, earlier):
    count, width = image_unit.shape
    rows = image.shape[0]
    return pl.pallas_call(
        loss_kernel,
        out_shape=(
            jax.ShapeDtypeStruct((count, width), F32),
            jax.ShapeDtypeStruct((3,), F32),
            jax.ShapeDtypeStruct((rows, width), BF16),
        ),
        in_specs=[SMEM] + [VMEM] * 4 + [SMEM] + [VMEM] * 2,
        out_specs=(VMEM, SMEM, VMEM),
        scratch_shapes=[
            pltpu.VMEM((rows, width), BF16),
            pltpu.VMEM((3, 8, max(rows, earlier[0].shape[0])), F32),
        ],
        input_output_aliases={4: 0},
        compiler_params=pltpu.CompilerParams(vmem_limit_bytes=VMEM_LIMIT),
        cost_estimate=cost(LOSS_FLOPS),
        name="loss_block",
    )(scal, image_unit, image, text, image_dunit, totals, *earlier)


def unit_kernel(scal, own, other, given, out):
    for rows in tiles(own.shape[0]):
        pair_grad = sigmoid_of(own[rows, :], other[...], scal[0], scal[1])
        out[rows, :] = given[rows, :] + weighted(pair_grad, other[...])


def raw_kernel(scal, own, raw, given, out, other):
    other[...] = unit_of(raw[...])
    unit_kernel(scal, own, other, given, out)


def side_block(scal, own, other, raw, dunit):
    return pl.pallas_call(
        raw_kernel if raw else unit_kernel,
        out_shape=jax.ShapeDtypeStruct(dunit.shape, F32),
        in_specs=[SMEM] + [VMEM] * 3,
        out_specs=VMEM,
        scratch_shapes=[pltpu.VMEM(other.shape, BF16)] * raw,
        input_output_aliases={3: 0},
        compiler_params=pltpu.CompilerParams(vmem_limit_bytes=VMEM_LIMIT),
        cost_estimate=cost(SIDE_FLOPS),
        name="side_block",
    )(scal, own, other, dunit)


def last_kernel(
    pair_count, scal, sums, image_own, text_own, image_unit, text_unit, image, text, image_in, text_in,
    image_grad, text_grad, loss, scalar_grads, other_image, other_text, image_out, text_out, sems,
):
    scale, bias = scal[0], scal[1]
    loss[0] = sums[0] * (1.0 / pair_count)
    scalar_grads[0] = scale * sums[1] * (1.0 / pair_count)
    scalar_grads[1] = sums[2] * (1.0 / pair_count)
    steps = image_own.shape[0] // LAST_TILE
    other_image[...] = unit_of(image[...])
    other_text[...] = unit_of(text[...])
    sides = (
        (image_own, image_unit, other_text, image_in, image_out, image_grad),
        (text_own, text_unit, other_image, text_in, text_out, text_grad),
    )
    copies = []
    for side, (own, unit, other, given, out, grad) in enumerate(sides):
        low = sigmoid_of(unit[...], other[...], scale, bias).astype(BF16)
        for step in range(steps):
            rows = slice(step * LAST_TILE, (step + 1) * LAST_TILE)
            dunit = given[rows, :] + jnp.dot(low[rows, :], other[...], preferred_element_type=F32)
            widened = own[rows, :].astype(F32)
            inverse = inverse_of(widened)
            along = jnp.sum(widened * dunit, axis=-1, keepdims=True) * inverse * inverse
            out[rows, :] = (dunit - widened * along) * (scale * inverse)
            copy = pltpu.make_async_copy(out.at[rows, :], grad.at[rows, :], sems.at[side, step])
            copy.start()
            copies.append(copy)
    for copy in copies:
        copy.wait()


def last_block(pair_count, scal, sums, image_own, text_own, image_unit, text_unit, image, text, image_dunit, text_dunit):
    count, width = image_own.shape
    rows = image.shape[0]
    grad = jax.ShapeDtypeStruct((count, width), F32)
    return pl.pallas_call(
        functools.partial(last_kernel, pair_count),
        out_shape=(grad, grad, jax.ShapeDtypeStruct((1,), F32), jax.ShapeDtypeStruct((2,), F32)),
        in_specs=[SMEM] * 2 + [VMEM] * 8,
        out_specs=(pl.BlockSpec(memory_space=pl.ANY), pl.BlockSpec(memory_space=pl.ANY), SMEM, SMEM),
        scratch_shapes=[
            pltpu.VMEM((rows, width), BF16),
            pltpu.VMEM((rows, width), BF16),
            pltpu.VMEM((count, width), F32),
            pltpu.VMEM((count, width), F32),
            pltpu.SemaphoreType.DMA((2, count // LAST_TILE)),
        ],
        compiler_params=pltpu.CompilerParams(vmem_limit_bytes=LAST_LIMIT),
        cost_estimate=cost(LAST_FLOPS),
        name="last_block",
    )(scal, sums, image_own, text_own, image_unit, text_unit, image, text, image_dunit, text_dunit)


def per_device(image_tower, text_tower, log_scale, bias):
    scal = jnp.concatenate([jnp.exp(log_scale), bias])
    back = functools.partial(passed_along, axis="blk", steps=-1)
    onward = functools.partial(passed_along, axis="blk", steps=1)
    image_a, text_a = back(image_tower[:SPLIT]), onward(text_tower[:SPLIT])
    image_b, text_b = back(image_tower[SPLIT:]), onward(text_tower[SPLIT:])
    image_unit, text_unit, image_dunit, text_dunit, totals = own_block(scal, image_tower, text_tower)

    image_a, text_a, image_dunit = lax.optimization_barrier((image_a, text_a, image_dunit))
    far = [(back(image_a), onward(text_a))]
    image_dunit, text_dunit, totals, *earlier = piece_block(
        scal, image_unit, text_unit, image_a, text_a, image_dunit, text_dunit, totals
    )
    image_b, text_b, image_dunit = lax.optimization_barrier((image_b, text_b, image_dunit))
    far += [(back(image_b[:PART]), onward(text_b[:PART])), (back(image_b[PART:]), onward(text_b[PART:]))]
    image_dunit, totals, image_b = loss_block(scal, image_unit, image_b, text_b, image_dunit, totals, earlier)

    def image_side(other):
        return lambda dunit: side_block(scal, image_unit, other, True, dunit)

    def text_side(other, raw=True):
        return lambda dunit: side_block(scal, text_unit, other, raw, dunit)

    totals, text_dunit = beside(totals, 0, text_dunit, text_side(image_b, False))
    totals = exchanged(totals, 1)
    totals, image_dunit = beside(totals, 2, image_dunit, image_side(far[0][1]))
    totals, text_dunit = beside(totals, 3, text_dunit, text_side(far[0][0]))
    totals = exchanged(totals, 4)
    totals, image_dunit = beside(totals, 5, image_dunit, image_side(far[1][1]))
    totals, text_dunit = beside(totals, 6, text_dunit, text_side(far[1][0]))
    pair_count = text_tower.shape[0] * lax.axis_size("outer") * lax.axis_size("blk")
    image_grad, text_grad, loss, scalar_grads = last_block(
        pair_count, scal, totals, image_tower, text_tower, image_unit, text_unit, *far[2], image_dunit, text_dunit
    )
    return (loss, image_grad, text_grad, scalar_grads)


def solution(mesh):
    return jax.shard_map(
        per_device,
        mesh=mesh,
        in_specs=(P(BOTH, None), P(BOTH, None), P(), P()),
        out_specs=(P(), P(BOTH, None), P(BOTH, None), P()),
        check_vma=False,
    )
```

```python
import functools

import functools

import jax
import jax.numpy as jnp
from jax import lax
from jax.experimental import pallas as pl
from jax.experimental.pallas import tpu as pltpu
from jax.sharding import PartitionSpec as P

F32 = jnp.float32
BF16 = jnp.bfloat16
TILE = 256
LAST_TILE = 128
SPLIT = 512
PART = 256
OWN_FLOPS = 3_000_000_000
PIECE_FLOPS = 1_000
LOSS_FLOPS = 20_000_000_000
SIDE_FLOPS = 3_000_000_000
LAST_FLOPS = 3_000_000_000
EXCHANGES = (("outer", 1), ("outer", 2), ("blk", 4), ("blk", 8), ("blk", 16), ("blk", 2), ("blk", 1))
SMEM = pl.BlockSpec(memory_space=pltpu.SMEM)
VMEM = pl.BlockSpec(memory_space=pltpu.VMEM)
VMEM_LIMIT = 24 * 1024 * 1024
LAST_LIMIT = 30 * 1024 * 1024
BOTH = ("outer", "blk")


def passed_along(value, axis, steps):
    count = lax.axis_size(axis)
    pairs = [(source, (source + steps) % count) for source in range(count)]
    return lax.ppermute(value, axis, pairs)


def exchanged(totals, step):
    axis, bit = EXCHANGES[step]
    pairs = [(source, source ^ bit) for source in range(lax.axis_size(axis))]
    return totals + lax.ppermute(totals, axis, pairs)


def beside(totals, step, dunit, work):
    totals, dunit = lax.optimization_barrier((totals, dunit))
    return lax.optimization_barrier((exchanged(totals, step), work(dunit)))


def cost(flops):
    return pl.CostEstimate(flops=flops, bytes_accessed=1_000_000, transcendentals=0)


def inverse_of(widened):
    return lax.rsqrt(jnp.sum(widened * widened, axis=-1, keepdims=True) + 1e-06)


def unit_of(tower):
    widened = tower.astype(F32)
    return (widened * inverse_of(widened)).astype(BF16)


def products(rows, others):
    return lax.dot_general(rows, others, (((1,), (1,)), ((), ())), preferred_element_type=F32)


def weighted(pair_grad, others):
    return jnp.dot(pair_grad.astype(BF16), others, preferred_element_type=F32)


def sigmoid_of(rows, others, scale, bias):
    return pl.reciprocal(1.0 + jnp.exp(-scale * products(rows, others) - bias))


def folded(values):
    return jnp.sum(values.reshape(values.shape[0] // 8, 8, values.shape[1]), axis=0)


def scored(sums, rows, others, scale, bias):
    cosine = products(rows, others)
    exped = jnp.exp(scale * cosine + bias)
    above = 1.0 + exped
    inverse = pl.reciprocal(above)
    pair_grad = exped * inverse
    width = others.shape[0]
    sums[0, :, :width] += folded(jnp.log(above) + (exped - (above - 1.0)) * inverse)
    sums[1, :, :width] += folded(pair_grad * cosine)
    sums[2, :, :width] += folded(pair_grad)
    return pair_grad


def tile_at(step):
    return pl.ds(pl.multiple_of(step * TILE, TILE), TILE)


def own_kernel(scal, image, text, image_unit, text_unit, image_dunit, text_dunit, totals, sums, grads):
    scale, bias = scal[0], scal[1]
    steps = image.shape[0] // TILE
    sums[...] = jnp.zeros_like(sums)

    @pl.loop(0, steps)
    def _(t):
        rows = tile_at(t)
        image_unit[rows, :] = unit_of(image[rows, :])
        text_unit[rows, :] = unit_of(text[rows, :])

    @pl.loop(0, steps)
    def _(t):
        rows = tile_at(t)
        cosine = products(image_unit[rows, :], text_unit[...])
        logit = scale * cosine + bias
        exped = jnp.exp(logit)
        pair_grad = exped / (1.0 + exped)
        diagonal = (
            lax.broadcasted_iota(jnp.int32, cosine.shape, 0) + t * TILE
            == lax.broadcasted_iota(jnp.int32, cosine.shape, 1)
        )
        pair_grad = jnp.where(diagonal, pair_grad - 1.0, pair_grad)
        sums[0] += folded(jnp.log1p(exped) - jnp.where(diagonal, logit, 0.0))
        sums[1] += folded(pair_grad * cosine)
        sums[2] += folded(pair_grad)
        grads[rows, :] = pair_grad.astype(BF16)
        image_dunit[rows, :] = weighted(pair_grad, text_unit[...])

    @pl.loop(0, steps)
    def _(t):
        rows = tile_at(t)
        text_dunit[rows, :] = lax.dot_general(
            grads[:, rows], image_unit[...], (((0,), (0,)), ((), ())), preferred_element_type=F32
        )

    for kind in range(3):
        totals[kind] = jnp.sum(sums[kind])


def own_block(scal, image, text):
    count, width = image.shape
    tower = jax.ShapeDtypeStruct((count, width), BF16)
    dunit = jax.ShapeDtypeStruct((count, width), F32)
    return pl.pallas_call(
        own_kernel,
        out_shape=(tower, tower, dunit, dunit, jax.ShapeDtypeStruct((3,), F32)),
        in_specs=[SMEM, VMEM, VMEM],
        out_specs=(VMEM, VMEM, VMEM, VMEM, SMEM),
        scratch_shapes=[pltpu.VMEM((3, 8, count), F32), pltpu.VMEM((count, count), BF16)],
        compiler_params=pltpu.CompilerParams(vmem_limit_bytes=VMEM_LIMIT),
        cost_estimate=cost(OWN_FLOPS),
        name="own_block",
    )(scal, image, text)


def tiles(count):
    return [slice(start, start + TILE) for start in range(0, count, TILE)]


def piece_kernel(
    scal, image_unit, text_unit, image, text, image_in, text_in, totals_in,
    image_dunit, text_dunit, totals, other_image, other_text, sums,
):
    scale, bias = scal[0], scal[1]
    other_image[...] = unit_of(image[...])
    other_text[...] = unit_of(text[...])
    sums[...] = jnp.zeros_like(sums)
    for rows in tiles(image_unit.shape[0]):
        pair_grad = scored(sums, image_unit[rows, :], other_text[...], scale, bias)
        image_dunit[rows, :] = image_in[rows, :] + weighted(pair_grad, other_text[...])
        pair_grad = sigmoid_of(text_unit[rows, :], other_image[...], scale, bias)
        text_dunit[rows, :] = text_in[rows, :] + weighted(pair_grad, other_image[...])
    for rows in tiles(other_image.shape[0]):
        scored(sums, other_image[rows, :], other_text[...], scale, bias)
    for kind in range(3):
        totals[kind] = totals_in[kind] + jnp.sum(sums[kind])


def piece_block(scal, image_unit, text_unit, image, text, image_dunit, text_dunit, totals):
    count, width = image_unit.shape
    rows = image.shape[0]
    dunit = jax.ShapeDtypeStruct((count, width), F32)
    unit = jax.ShapeDtypeStruct((rows, width), BF16)
    return pl.pallas_call(
        piece_kernel,
        out_shape=(dunit, dunit, jax.ShapeDtypeStruct((3,), F32), unit, unit),
        in_specs=[SMEM] + [VMEM] * 6 + [SMEM],
        out_specs=(VMEM, VMEM, SMEM, VMEM, VMEM),
        scratch_shapes=[pltpu.VMEM((3, 8, rows), F32)],
        input_output_aliases={5: 0, 6: 1},
        compiler_params=pltpu.CompilerParams(vmem_limit_bytes=VMEM_LIMIT),
        cost_estimate=cost(PIECE_FLOPS),
        name="piece_block",
    )(scal, image_unit, text_unit, image, text, image_dunit, text_dunit, totals)


def loss_kernel(
    scal, image_unit, image, text, image_in, totals_in, image_before, text_before,
    image_dunit, totals, other_image, other_text, sums,
):
    scale, bias = scal[0], scal[1]
    other_image[...] = unit_of(image[...])
    other_text[...] = unit_of(text[...])
    sums[...] = jnp.zeros_like(sums)
    for rows in tiles(image_unit.shape[0]):
        pair_grad = scored(sums, image_unit[rows, :], other_text[...], scale, bias)
        image_dunit[rows, :] = image_in[rows, :] + weighted(pair_grad, other_text[...])
    for rows in tiles(other_image.shape[0]):
        for text_units in (other_text, text_before):
            scored(sums, other_image[rows, :], text_units[...], scale, bias)
    for rows in tiles(image_before.shape[0]):
        scored(sums, image_before[rows, :], other_text[...], scale, bias)
    for kind in range(3):
        totals[kind] = totals_in[kind] + jnp.sum(sums[kind])


def loss_block(scal, image_unit, image, text, image_dunit, totals, earlier):
    count, width = image_unit.shape
    rows = image.shape[0]
    return pl.pallas_call(
        loss_kernel,
        out_shape=(
            jax.ShapeDtypeStruct((count, width), F32),
            jax.ShapeDtypeStruct((3,), F32),
            jax.ShapeDtypeStruct((rows, width), BF16),
        ),
        in_specs=[SMEM] + [VMEM] * 4 + [SMEM] + [VMEM] * 2,
        out_specs=(VMEM, SMEM, VMEM),
        scratch_shapes=[
            pltpu.VMEM((rows, width), BF16),
            pltpu.VMEM((3, 8, max(rows, earlier[0].shape[0])), F32),
        ],
        input_output_aliases={4: 0},
        compiler_params=pltpu.CompilerParams(vmem_limit_bytes=VMEM_LIMIT),
        cost_estimate=cost(LOSS_FLOPS),
        name="loss_block",
    )(scal, image_unit, image, text, image_dunit, totals, *earlier)


def unit_kernel(half, scal, own, other, given, out):
    for rows in halves(own.shape[0])[half]:
        pair_grad = sigmoid_of(own[rows, :], other[...], scal[0], scal[1])
        out[rows, :] = given[rows, :] + weighted(pair_grad, other[...])


def raw_kernel(half, scal, own, raw, given, out, other):
    other[...] = unit_of(raw[...])
    unit_kernel(half, scal, own, other, given, out)


def halves(count):
    every = tiles(count)
    middle = len(every) // 2
    return every[:middle], every[middle:], every


def side_block(scal, own, other, raw, half, dunit):
    shapes = [jax.ShapeDtypeStruct(dunit.shape, F32)]
    if raw:
        shapes.append(jax.ShapeDtypeStruct(other.shape, BF16))
    return pl.pallas_call(
        functools.partial(raw_kernel if raw else unit_kernel, half),
        out_shape=shapes,
        in_specs=[SMEM] + [VMEM] * 3,
        out_specs=[VMEM] * len(shapes),
        input_output_aliases={3: 0},
        compiler_params=pltpu.CompilerParams(vmem_limit_bytes=VMEM_LIMIT),
        cost_estimate=cost(SIDE_FLOPS),
        name="side_block",
    )(scal, own, other, dunit)


def last_kernel(
    pair_count, scal, sums, image_own, text_own, image_unit, text_unit, image, text, image_in, text_in,
    image_grad, text_grad, loss, scalar_grads, other_image, other_text, image_out, text_out, sems,
):
    scale, bias = scal[0], scal[1]
    loss[0] = sums[0] * (1.0 / pair_count)
    scalar_grads[0] = scale * sums[1] * (1.0 / pair_count)
    scalar_grads[1] = sums[2] * (1.0 / pair_count)
    steps = image_own.shape[0] // LAST_TILE
    other_image[...] = unit_of(image[...])
    other_text[...] = unit_of(text[...])
    sides = (
        (image_own, image_unit, other_text, image_in, image_out, image_grad),
        (text_own, text_unit, other_image, text_in, text_out, text_grad),
    )
    copies = []
    for side, (own, unit, other, given, out, grad) in enumerate(sides):
        low = sigmoid_of(unit[...], other[...], scale, bias).astype(BF16)
        for step in range(steps):
            rows = slice(step * LAST_TILE, (step + 1) * LAST_TILE)
            dunit = given[rows, :] + jnp.dot(low[rows, :], other[...], preferred_element_type=F32)
            widened = own[rows, :].astype(F32)
            inverse = inverse_of(widened)
            along = jnp.sum(widened * dunit, axis=-1, keepdims=True) * inverse * inverse
            out[rows, :] = (dunit - widened * along) * (scale * inverse)
            copy = pltpu.make_async_copy(out.at[rows, :], grad.at[rows, :], sems.at[side, step])
            copy.start()
            copies.append(copy)
    for copy in copies:
        copy.wait()


def last_block(pair_count, scal, sums, image_own, text_own, image_unit, text_unit, image, text, image_dunit, text_dunit):
    count, width = image_own.shape
    rows = image.shape[0]
    grad = jax.ShapeDtypeStruct((count, width), F32)
    return pl.pallas_call(
        functools.partial(last_kernel, pair_count),
        out_shape=(grad, grad, jax.ShapeDtypeStruct((1,), F32), jax.ShapeDtypeStruct((2,), F32)),
        in_specs=[SMEM] * 2 + [VMEM] * 8,
        out_specs=(pl.BlockSpec(memory_space=pl.ANY), pl.BlockSpec(memory_space=pl.ANY), SMEM, SMEM),
        scratch_shapes=[
            pltpu.VMEM((rows, width), BF16),
            pltpu.VMEM((rows, width), BF16),
            pltpu.VMEM((count, width), F32),
            pltpu.VMEM((count, width), F32),
            pltpu.SemaphoreType.DMA((2, count // LAST_TILE)),
        ],
        compiler_params=pltpu.CompilerParams(vmem_limit_bytes=LAST_LIMIT),
        cost_estimate=cost(LAST_FLOPS),
        name="last_block",
    )(scal, sums, image_own, text_own, image_unit, text_unit, image, text, image_dunit, text_dunit)


def per_device(image_tower, text_tower, log_scale, bias):
    scal = jnp.concatenate([jnp.exp(log_scale), bias])
    back = functools.partial(passed_along, axis="blk", steps=-1)
    onward = functools.partial(passed_along, axis="blk", steps=1)
    image_a, text_a = back(image_tower[:SPLIT]), onward(text_tower[:SPLIT])
    image_b, text_b = back(image_tower[SPLIT:]), onward(text_tower[SPLIT:])
    image_unit, text_unit, image_dunit, text_dunit, totals = own_block(scal, image_tower, text_tower)

    image_a, text_a, image_dunit = lax.optimization_barrier((image_a, text_a, image_dunit))
    far = [(back(image_a), onward(text_a))]
    image_dunit, text_dunit, totals, *earlier = piece_block(
        scal, image_unit, text_unit, image_a, text_a, image_dunit, text_dunit, totals
    )
    image_b, text_b, image_dunit = lax.optimization_barrier((image_b, text_b, image_dunit))
    far.append((back(image_b[:PART]), onward(text_b[:PART])))
    rear = (image_b[PART:], text_b[PART:])
    image_dunit, totals, image_b = loss_block(scal, image_unit, image_b, text_b, image_dunit, totals, earlier)

    def first_half(own, raw):
        return lambda dunit: side_block(scal, own, raw, True, 0, dunit)

    def other_half(own, unit, half=1):
        return lambda dunit: side_block(scal, own, unit, False, half, dunit)

    (far_image, far_text), (near_image, near_text) = far
    totals, (text_dunit,) = beside(totals, 0, text_dunit, other_half(text_unit, image_b, 0))
    totals, (text_dunit,) = beside(totals, 1, text_dunit, other_half(text_unit, image_b))
    totals, rear = lax.optimization_barrier((totals, rear))
    rear = (back(rear[0]), onward(rear[1]))
    totals, (image_dunit, far_text) = beside(totals, 2, image_dunit, first_half(image_unit, far_text))
    totals, (image_dunit,) = beside(totals, 3, image_dunit, other_half(image_unit, far_text))
    totals, (text_dunit, far_image) = beside(totals, 4, text_dunit, first_half(text_unit, far_image))
    totals, (text_dunit,) = beside(totals, 5, text_dunit, other_half(text_unit, far_image))
    totals, (image_dunit, _) = beside(totals, 6, image_dunit, lambda d: side_block(scal, image_unit, near_text, True, 2, d))
    text_dunit, _ = side_block(scal, text_unit, near_image, True, 2, text_dunit)
    pair_count = text_tower.shape[0] * lax.axis_size("outer") * lax.axis_size("blk")
    image_grad, text_grad, loss, scalar_grads = last_block(
        pair_count, scal, totals, image_tower, text_tower, image_unit, text_unit, *rear, image_dunit, text_dunit
    )
    return (loss, image_grad, text_grad, scalar_grads)


def solution(mesh):
    return jax.shard_map(
        per_device,
        mesh=mesh,
        in_specs=(P(BOTH, None), P(BOTH, None), P(), P()),
        out_specs=(P(), P(BOTH, None), P(BOTH, None), P()),
        check_vma=False,
    )
```

```python
import functools

import functools

import jax
import jax.numpy as jnp
from jax import lax
from jax.experimental import pallas as pl
from jax.experimental.pallas import tpu as pltpu
from jax.sharding import PartitionSpec as P

F32 = jnp.float32
BF16 = jnp.bfloat16
TILE = 256
LAST_TILE = 128
SPLIT = 512
PART = 256
OWN_FLOPS = 3_000_000_000
PIECE_FLOPS = 1_000
LOSS_FLOPS = 20_000_000_000
SIDE_FLOPS = 3_000_000_000
LAST_FLOPS = 3_000_000_000
EXCHANGES = (("outer", 1), ("outer", 2), ("blk", 4), ("blk", 8), ("blk", 16), ("blk", 2), ("blk", 1))
SMEM = pl.BlockSpec(memory_space=pltpu.SMEM)
VMEM = pl.BlockSpec(memory_space=pltpu.VMEM)
VMEM_LIMIT = 24 * 1024 * 1024
LAST_LIMIT = 30 * 1024 * 1024
BOTH = ("outer", "blk")


def passed_along(value, axis, steps):
    count = lax.axis_size(axis)
    pairs = [(source, (source + steps) % count) for source in range(count)]
    return lax.ppermute(value, axis, pairs)


def exchanged(totals, step):
    axis, bit = EXCHANGES[step]
    pairs = [(source, source ^ bit) for source in range(lax.axis_size(axis))]
    return totals + lax.ppermute(totals, axis, pairs)


def beside(totals, step, dunit, work):
    totals, dunit = lax.optimization_barrier((totals, dunit))
    return lax.optimization_barrier((exchanged(totals, step), work(dunit)))


def cost(flops):
    return pl.CostEstimate(flops=flops, bytes_accessed=1_000_000, transcendentals=0)


def inverse_of(widened):
    return lax.rsqrt(jnp.sum(widened * widened, axis=-1, keepdims=True) + 1e-06)


def unit_of(tower):
    widened = tower.astype(F32)
    return (widened * inverse_of(widened)).astype(BF16)


def products(rows, others):
    return lax.dot_general(rows, others, (((1,), (1,)), ((), ())), preferred_element_type=F32)


def weighted(pair_grad, others):
    return jnp.dot(pair_grad.astype(BF16), others, preferred_element_type=F32)


def sigmoid_of(rows, others, scale, bias):
    return pl.reciprocal(1.0 + jnp.exp(-scale * products(rows, others) - bias))


def folded(values):
    return jnp.sum(values.reshape(values.shape[0] // 8, 8, values.shape[1]), axis=0)


def scored(sums, rows, others, scale, bias):
    cosine = products(rows, others)
    exped = jnp.exp(scale * cosine + bias)
    above = 1.0 + exped
    inverse = pl.reciprocal(above)
    pair_grad = exped * inverse
    width = others.shape[0]
    sums[0, :, :width] += folded(jnp.log(above) + (exped - (above - 1.0)) * inverse)
    sums[1, :, :width] += folded(pair_grad * cosine)
    sums[2, :, :width] += folded(pair_grad)
    return pair_grad


def tile_at(step):
    return pl.ds(pl.multiple_of(step * TILE, TILE), TILE)


def own_kernel(scal, image, text, image_unit, text_unit, image_dunit, text_dunit, totals, sums, grads):
    scale, bias = scal[0], scal[1]
    steps = image.shape[0] // TILE
    sums[...] = jnp.zeros_like(sums)

    @pl.loop(0, steps)
    def _(t):
        rows = tile_at(t)
        image_unit[rows, :] = unit_of(image[rows, :])
        text_unit[rows, :] = unit_of(text[rows, :])

    @pl.loop(0, steps)
    def _(t):
        rows = tile_at(t)
        cosine = products(image_unit[rows, :], text_unit[...])
        logit = scale * cosine + bias
        exped = jnp.exp(logit)
        pair_grad = exped / (1.0 + exped)
        diagonal = (
            lax.broadcasted_iota(jnp.int32, cosine.shape, 0) + t * TILE
            == lax.broadcasted_iota(jnp.int32, cosine.shape, 1)
        )
        pair_grad = jnp.where(diagonal, pair_grad - 1.0, pair_grad)
        sums[0] += folded(jnp.log1p(exped) - jnp.where(diagonal, logit, 0.0))
        sums[1] += folded(pair_grad * cosine)
        sums[2] += folded(pair_grad)
        grads[rows, :] = pair_grad.astype(BF16)
        image_dunit[rows, :] = weighted(pair_grad, text_unit[...])

    @pl.loop(0, steps)
    def _(t):
        rows = tile_at(t)
        text_dunit[rows, :] = lax.dot_general(
            grads[:, rows], image_unit[...], (((0,), (0,)), ((), ())), preferred_element_type=F32
        )

    for kind in range(3):
        totals[kind] = jnp.sum(sums[kind])


def own_block(scal, image, text):
    count, width = image.shape
    tower = jax.ShapeDtypeStruct((count, width), BF16)
    dunit = jax.ShapeDtypeStruct((count, width), F32)
    return pl.pallas_call(
        own_kernel,
        out_shape=(tower, tower, dunit, dunit, jax.ShapeDtypeStruct((3,), F32)),
        in_specs=[SMEM, VMEM, VMEM],
        out_specs=(VMEM, VMEM, VMEM, VMEM, SMEM),
        scratch_shapes=[pltpu.VMEM((3, 8, count), F32), pltpu.VMEM((count, count), BF16)],
        compiler_params=pltpu.CompilerParams(vmem_limit_bytes=VMEM_LIMIT),
        cost_estimate=cost(OWN_FLOPS),
        name="own_block",
    )(scal, image, text)


def tiles(count):
    return [slice(start, start + TILE) for start in range(0, count, TILE)]


def piece_kernel(
    scal, image_unit, text_unit, image, text, image_in, text_in, totals_in,
    image_dunit, text_dunit, totals, other_image, other_text, sums,
):
    scale, bias = scal[0], scal[1]
    other_image[...] = unit_of(image[...])
    other_text[...] = unit_of(text[...])
    sums[...] = jnp.zeros_like(sums)
    for rows in tiles(image_unit.shape[0]):
        pair_grad = scored(sums, image_unit[rows, :], other_text[...], scale, bias)
        image_dunit[rows, :] = image_in[rows, :] + weighted(pair_grad, other_text[...])
        pair_grad = sigmoid_of(text_unit[rows, :], other_image[...], scale, bias)
        text_dunit[rows, :] = text_in[rows, :] + weighted(pair_grad, other_image[...])
    for rows in tiles(other_image.shape[0]):
        scored(sums, other_image[rows, :], other_text[...], scale, bias)
    for kind in range(3):
        totals[kind] = totals_in[kind] + jnp.sum(sums[kind])


def piece_block(scal, image_unit, text_unit, image, text, image_dunit, text_dunit, totals):
    count, width = image_unit.shape
    rows = image.shape[0]
    dunit = jax.ShapeDtypeStruct((count, width), F32)
    unit = jax.ShapeDtypeStruct((rows, width), BF16)
    return pl.pallas_call(
        piece_kernel,
        out_shape=(dunit, dunit, jax.ShapeDtypeStruct((3,), F32), unit, unit),
        in_specs=[SMEM] + [VMEM] * 6 + [SMEM],
        out_specs=(VMEM, VMEM, SMEM, VMEM, VMEM),
        scratch_shapes=[pltpu.VMEM((3, 8, rows), F32)],
        input_output_aliases={5: 0, 6: 1},
        compiler_params=pltpu.CompilerParams(vmem_limit_bytes=VMEM_LIMIT),
        cost_estimate=cost(PIECE_FLOPS),
        name="piece_block",
    )(scal, image_unit, text_unit, image, text, image_dunit, text_dunit, totals)


def loss_kernel(
    scal, image_unit, image, text, image_in, totals_in, image_before, text_before,
    image_dunit, totals, other_image, other_text, sums,
):
    scale, bias = scal[0], scal[1]
    other_image[...] = unit_of(image[...])
    other_text[...] = unit_of(text[...])
    sums[...] = jnp.zeros_like(sums)
    for rows in tiles(image_unit.shape[0]):
        pair_grad = scored(sums, image_unit[rows, :], other_text[...], scale, bias)
        image_dunit[rows, :] = image_in[rows, :] + weighted(pair_grad, other_text[...])
    for rows in tiles(other_image.shape[0]):
        for text_units in (other_text, text_before):
            scored(sums, other_image[rows, :], text_units[...], scale, bias)
    for rows in tiles(image_before.shape[0]):
        scored(sums, image_before[rows, :], other_text[...], scale, bias)
    for kind in range(3):
        totals[kind] = totals_in[kind] + jnp.sum(sums[kind])


def loss_block(scal, image_unit, image, text, image_dunit, totals, earlier):
    count, width = image_unit.shape
    rows = image.shape[0]
    return pl.pallas_call(
        loss_kernel,
        out_shape=(
            jax.ShapeDtypeStruct((count, width), F32),
            jax.ShapeDtypeStruct((3,), F32),
            jax.ShapeDtypeStruct((rows, width), BF16),
        ),
        in_specs=[SMEM] + [VMEM] * 4 + [SMEM] + [VMEM] * 2,
        out_specs=(VMEM, SMEM, VMEM),
        scratch_shapes=[
            pltpu.VMEM((rows, width), BF16),
            pltpu.VMEM((3, 8, max(rows, earlier[0].shape[0])), F32),
        ],
        input_output_aliases={4: 0},
        compiler_params=pltpu.CompilerParams(vmem_limit_bytes=VMEM_LIMIT),
        cost_estimate=cost(LOSS_FLOPS),
        name="loss_block",
    )(scal, image_unit, image, text, image_dunit, totals, *earlier)


def unit_kernel(half, scal, own, other, given, out):
    for rows in halves(own.shape[0])[half]:
        pair_grad = sigmoid_of(own[rows, :], other[...], scal[0], scal[1])
        out[rows, :] = given[rows, :] + weighted(pair_grad, other[...])


def raw_kernel(half, scal, own, raw, given, out, other):
    other[...] = unit_of(raw[...])
    unit_kernel(half, scal, own, other, given, out)


def halves(count):
    every = tiles(count)
    middle = len(every) // 2
    return every[:middle], every[middle:], every


def side_block(scal, own, other, raw, half, dunit):
    shapes = [jax.ShapeDtypeStruct(dunit.shape, F32)]
    if raw:
        shapes.append(jax.ShapeDtypeStruct(other.shape, BF16))
    return pl.pallas_call(
        functools.partial(raw_kernel if raw else unit_kernel, half),
        out_shape=shapes,
        in_specs=[SMEM] + [VMEM] * 3,
        out_specs=[VMEM] * len(shapes),
        input_output_aliases={3: 0},
        compiler_params=pltpu.CompilerParams(vmem_limit_bytes=VMEM_LIMIT),
        cost_estimate=cost(SIDE_FLOPS),
        name="side_block",
    )(scal, own, other, dunit)


def last_kernel(
    pair_count, scal, sums, image_own, text_own, image_unit, text_unit, image, text, image_in, text_in,
    image_grad, text_grad, loss, scalar_grads, other_image, other_text, image_out, text_out, sems,
):
    scale, bias = scal[0], scal[1]
    loss[0] = sums[0] * (1.0 / pair_count)
    scalar_grads[0] = scale * sums[1] * (1.0 / pair_count)
    scalar_grads[1] = sums[2] * (1.0 / pair_count)
    steps = image_own.shape[0] // LAST_TILE
    other_image[...] = unit_of(image[...])
    other_text[...] = unit_of(text[...])
    sides = (
        (image_own, image_unit, other_text, image_in, image_out, image_grad),
        (text_own, text_unit, other_image, text_in, text_out, text_grad),
    )
    copies = []
    for side, (own, unit, other, given, out, grad) in enumerate(sides):
        low = sigmoid_of(unit[...], other[...], scale, bias).astype(BF16)
        for step in range(steps):
            rows = slice(step * LAST_TILE, (step + 1) * LAST_TILE)
            dunit = given[rows, :] + jnp.dot(low[rows, :], other[...], preferred_element_type=F32)
            widened = own[rows, :].astype(F32)
            inverse = inverse_of(widened)
            along = jnp.sum(widened * dunit, axis=-1, keepdims=True) * inverse * inverse
            out[rows, :] = (dunit - widened * along) * (scale * inverse)
            copy = pltpu.make_async_copy(out.at[rows, :], grad.at[rows, :], sems.at[side, step])
            copy.start()
            copies.append(copy)
    for copy in copies:
        copy.wait()


def last_block(pair_count, scal, sums, image_own, text_own, image_unit, text_unit, image, text, image_dunit, text_dunit):
    count, width = image_own.shape
    rows = image.shape[0]
    grad = jax.ShapeDtypeStruct((count, width), F32)
    return pl.pallas_call(
        functools.partial(last_kernel, pair_count),
        out_shape=(grad, grad, jax.ShapeDtypeStruct((1,), F32), jax.ShapeDtypeStruct((2,), F32)),
        in_specs=[SMEM] * 2 + [VMEM] * 8,
        out_specs=(pl.BlockSpec(memory_space=pl.ANY), pl.BlockSpec(memory_space=pl.ANY), SMEM, SMEM),
        scratch_shapes=[
            pltpu.VMEM((rows, width), BF16),
            pltpu.VMEM((rows, width), BF16),
            pltpu.VMEM((count, width), F32),
            pltpu.VMEM((count, width), F32),
            pltpu.SemaphoreType.DMA((2, count // LAST_TILE)),
        ],
        compiler_params=pltpu.CompilerParams(vmem_limit_bytes=LAST_LIMIT),
        cost_estimate=cost(LAST_FLOPS),
        name="last_block",
    )(scal, sums, image_own, text_own, image_unit, text_unit, image, text, image_dunit, text_dunit)


def per_device(image_tower, text_tower, log_scale, bias):
    scal = jnp.concatenate([jnp.exp(log_scale), bias])
    back = functools.partial(passed_along, axis="blk", steps=-1)
    onward = functools.partial(passed_along, axis="blk", steps=1)
    text_a, image_a = onward(text_tower[:SPLIT]), back(image_tower[:SPLIT])
    image_rest, text_rest = lax.optimization_barrier((image_tower, text_tower))
    text_b, image_b = onward(text_rest[SPLIT:]), back(image_rest[SPLIT:])
    image_unit, text_unit, image_dunit, text_dunit, totals = own_block(scal, image_tower, text_tower)

    image_a, text_a, image_dunit = lax.optimization_barrier((image_a, text_a, image_dunit))
    far = [(back(image_a), onward(text_a))]
    image_dunit, text_dunit, totals, *earlier = piece_block(
        scal, image_unit, text_unit, image_a, text_a, image_dunit, text_dunit, totals
    )
    image_b, text_b, image_dunit = lax.optimization_barrier((image_b, text_b, image_dunit))
    far.append((back(image_b[:PART]), onward(text_b[:PART])))
    rear = (image_b[PART:], text_b[PART:])
    image_dunit, totals, image_b = loss_block(scal, image_unit, image_b, text_b, image_dunit, totals, earlier)

    def first_half(own, raw):
        return lambda dunit: side_block(scal, own, raw, True, 0, dunit)

    def other_half(own, unit, half=1):
        return lambda dunit: side_block(scal, own, unit, False, half, dunit)

    (far_image, far_text), (near_image, near_text) = far
    totals = exchanged(totals, 0)
    totals, (text_dunit,) = beside(totals, 1, text_dunit, other_half(text_unit, image_b, 0))
    totals, (text_dunit,) = beside(totals, 2, text_dunit, other_half(text_unit, image_b))
    totals, rear = lax.optimization_barrier((totals, rear))
    rear = (back(rear[0]), onward(rear[1]))
    totals, (image_dunit, far_text) = beside(totals, 3, image_dunit, first_half(image_unit, far_text))
    totals, (image_dunit,) = beside(totals, 4, image_dunit, other_half(image_unit, far_text))
    totals, (text_dunit, far_image) = beside(totals, 5, text_dunit, first_half(text_unit, far_image))
    totals, (text_dunit,) = beside(totals, 6, text_dunit, other_half(text_unit, far_image))
    image_dunit, _ = side_block(scal, image_unit, near_text, True, 2, image_dunit)
    text_dunit, _ = side_block(scal, text_unit, near_image, True, 2, text_dunit)
    pair_count = text_tower.shape[0] * lax.axis_size("outer") * lax.axis_size("blk")
    image_grad, text_grad, loss, scalar_grads = last_block(
        pair_count, scal, totals, image_tower, text_tower, image_unit, text_unit, *rear, image_dunit, text_dunit
    )
    return (loss, image_grad, text_grad, scalar_grads)


def solution(mesh):
    return jax.shard_map(
        per_device,
        mesh=mesh,
        in_specs=(P(BOTH, None), P(BOTH, None), P(), P()),
        out_specs=(P(), P(BOTH, None), P(BOTH, None), P()),
        check_vma=False,
    )
```

```python
import functools

import functools

import jax
import jax.numpy as jnp
from jax import lax
from jax.experimental import pallas as pl
from jax.experimental.pallas import tpu as pltpu
from jax.sharding import PartitionSpec as P

F32 = jnp.float32
BF16 = jnp.bfloat16
TILE = 256
LAST_TILE = 128
ENDS = (512, 768)
OWN_FLOPS = 3_000_000_000
PIECE_FLOPS = 1_000
LOSS_FLOPS = 20_000_000_000
SIDE_FLOPS = 3_000_000_000
LAST_FLOPS = 3_000_000_000
EXCHANGES = (("outer", 1), ("outer", 2), ("blk", 4), ("blk", 8), ("blk", 16), ("blk", 2), ("blk", 1))
SMEM = pl.BlockSpec(memory_space=pltpu.SMEM)
VMEM = pl.BlockSpec(memory_space=pltpu.VMEM)
VMEM_LIMIT = 24 * 1024 * 1024
LAST_LIMIT = 30 * 1024 * 1024
BOTH = ("outer", "blk")


def passed_along(value, axis, steps):
    count = lax.axis_size(axis)
    pairs = [(source, (source + steps) % count) for source in range(count)]
    return lax.ppermute(value, axis, pairs)


def exchanged(totals, step):
    axis, bit = EXCHANGES[step]
    pairs = [(source, source ^ bit) for source in range(lax.axis_size(axis))]
    return totals + lax.ppermute(totals, axis, pairs)


def beside(totals, step, dunit, work):
    totals, dunit = lax.optimization_barrier((totals, dunit))
    return lax.optimization_barrier((exchanged(totals, step), work(dunit)))


def cost(flops):
    return pl.CostEstimate(flops=flops, bytes_accessed=1_000_000, transcendentals=0)


def inverse_of(widened):
    return lax.rsqrt(jnp.sum(widened * widened, axis=-1, keepdims=True) + 1e-06)


def unit_of(tower):
    widened = tower.astype(F32)
    return (widened * inverse_of(widened)).astype(BF16)


def products(rows, others):
    return lax.dot_general(rows, others, (((1,), (1,)), ((), ())), preferred_element_type=F32)


def weighted(pair_grad, others):
    return jnp.dot(pair_grad.astype(BF16), others, preferred_element_type=F32)


def sigmoid_of(rows, others, scale, bias):
    return pl.reciprocal(1.0 + jnp.exp(-scale * products(rows, others) - bias))


def folded(values):
    return jnp.sum(values.reshape(values.shape[0] // 8, 8, values.shape[1]), axis=0)


def scored(sums, rows, others, scale, bias):
    cosine = products(rows, others)
    exped = jnp.exp(scale * cosine + bias)
    above = 1.0 + exped
    inverse = pl.reciprocal(above)
    pair_grad = exped * inverse
    width = others.shape[0]
    sums[0, :, :width] += folded(jnp.log(above) + (exped - (above - 1.0)) * inverse)
    sums[1, :, :width] += folded(pair_grad * cosine)
    sums[2, :, :width] += folded(pair_grad)
    return pair_grad


def tile_at(step):
    return pl.ds(pl.multiple_of(step * TILE, TILE), TILE)


def own_kernel(scal, image, text, image_unit, text_unit, image_dunit, text_dunit, totals, sums, grads):
    scale, bias = scal[0], scal[1]
    steps = image.shape[0] // TILE
    sums[...] = jnp.zeros_like(sums)

    @pl.loop(0, steps)
    def _(t):
        rows = tile_at(t)
        image_unit[rows, :] = unit_of(image[rows, :])
        text_unit[rows, :] = unit_of(text[rows, :])

    @pl.loop(0, steps)
    def _(t):
        rows = tile_at(t)
        cosine = products(image_unit[rows, :], text_unit[...])
        logit = scale * cosine + bias
        exped = jnp.exp(logit)
        pair_grad = exped / (1.0 + exped)
        diagonal = (
            lax.broadcasted_iota(jnp.int32, cosine.shape, 0) + t * TILE
            == lax.broadcasted_iota(jnp.int32, cosine.shape, 1)
        )
        pair_grad = jnp.where(diagonal, pair_grad - 1.0, pair_grad)
        sums[0] += folded(jnp.log1p(exped) - jnp.where(diagonal, logit, 0.0))
        sums[1] += folded(pair_grad * cosine)
        sums[2] += folded(pair_grad)
        grads[rows, :] = pair_grad.astype(BF16)
        image_dunit[rows, :] = weighted(pair_grad, text_unit[...])

    @pl.loop(0, steps)
    def _(t):
        rows = tile_at(t)
        text_dunit[rows, :] = lax.dot_general(
            grads[:, rows], image_unit[...], (((0,), (0,)), ((), ())), preferred_element_type=F32
        )

    for kind in range(3):
        totals[kind] = jnp.sum(sums[kind])


def own_block(scal, image, text):
    count, width = image.shape
    tower = jax.ShapeDtypeStruct((count, width), BF16)
    dunit = jax.ShapeDtypeStruct((count, width), F32)
    return pl.pallas_call(
        own_kernel,
        out_shape=(tower, tower, dunit, dunit, jax.ShapeDtypeStruct((3,), F32)),
        in_specs=[SMEM, VMEM, VMEM],
        out_specs=(VMEM, VMEM, VMEM, VMEM, SMEM),
        scratch_shapes=[pltpu.VMEM((3, 8, count), F32), pltpu.VMEM((count, count), BF16)],
        compiler_params=pltpu.CompilerParams(vmem_limit_bytes=VMEM_LIMIT),
        cost_estimate=cost(OWN_FLOPS),
        name="own_block",
    )(scal, image, text)


def tiles(count):
    return [slice(start, start + TILE) for start in range(0, count, TILE)]


def cross_scored(sums, other_image, other_text, image_before, text_before, scale, bias):
    for rows in tiles(other_image.shape[0]):
        for text_units in (other_text, *text_before):
            scored(sums, other_image[rows, :], text_units[...], scale, bias)
    for image_units in image_before:
        for rows in tiles(image_units.shape[0]):
            scored(sums, image_units[rows, :], other_text[...], scale, bias)


def piece_kernel(before, scal, image_unit, text_unit, image, text, image_in, text_in, totals_in, *rest):
    image_before, text_before = rest[:before], rest[before : 2 * before]
    image_dunit, text_dunit, totals, other_image, other_text, sums = rest[2 * before :]
    scale, bias = scal[0], scal[1]
    other_image[...] = unit_of(image[...])
    other_text[...] = unit_of(text[...])
    sums[...] = jnp.zeros_like(sums)
    for rows in tiles(image_unit.shape[0]):
        pair_grad = scored(sums, image_unit[rows, :], other_text[...], scale, bias)
        image_dunit[rows, :] = image_in[rows, :] + weighted(pair_grad, other_text[...])
        pair_grad = sigmoid_of(text_unit[rows, :], other_image[...], scale, bias)
        text_dunit[rows, :] = text_in[rows, :] + weighted(pair_grad, other_image[...])
    cross_scored(sums, other_image, other_text, image_before, text_before, scale, bias)
    for kind in range(3):
        totals[kind] = totals_in[kind] + jnp.sum(sums[kind])


def piece_block(scal, image_unit, text_unit, image, text, image_dunit, text_dunit, totals, earlier):
    count, width = image_unit.shape
    rows = image.shape[0]
    dunit = jax.ShapeDtypeStruct((count, width), F32)
    unit = jax.ShapeDtypeStruct((rows, width), BF16)
    before = [pair[side] for side in (0, 1) for pair in earlier]
    broad = max(piece.shape[0] for piece in [image, *before])
    return pl.pallas_call(
        functools.partial(piece_kernel, len(earlier)),
        out_shape=(dunit, dunit, jax.ShapeDtypeStruct((3,), F32), unit, unit),
        in_specs=[SMEM] + [VMEM] * 6 + [SMEM] + [VMEM] * len(before),
        out_specs=(VMEM, VMEM, SMEM, VMEM, VMEM),
        scratch_shapes=[pltpu.VMEM((3, 8, broad), F32)],
        input_output_aliases={5: 0, 6: 1},
        compiler_params=pltpu.CompilerParams(vmem_limit_bytes=VMEM_LIMIT),
        cost_estimate=cost(PIECE_FLOPS),
        name="piece_block",
    )(scal, image_unit, text_unit, image, text, image_dunit, text_dunit, totals, *before)


def loss_kernel(before, scal, image_unit, image, text, image_in, totals_in, *rest):
    image_before, text_before = rest[:before], rest[before : 2 * before]
    image_dunit, totals, other_image, other_text, sums = rest[2 * before :]
    scale, bias = scal[0], scal[1]
    other_image[...] = unit_of(image[...])
    other_text[...] = unit_of(text[...])
    sums[...] = jnp.zeros_like(sums)
    for rows in tiles(image_unit.shape[0]):
        pair_grad = scored(sums, image_unit[rows, :], other_text[...], scale, bias)
        image_dunit[rows, :] = image_in[rows, :] + weighted(pair_grad, other_text[...])
    cross_scored(sums, other_image, other_text, image_before, text_before, scale, bias)
    for kind in range(3):
        totals[kind] = totals_in[kind] + jnp.sum(sums[kind])


def loss_block(scal, image_unit, image, text, image_dunit, totals, earlier):
    count, width = image_unit.shape
    rows = image.shape[0]
    before = [pair[side] for side in (0, 1) for pair in earlier]
    broad = max(piece.shape[0] for piece in [image, *before])
    return pl.pallas_call(
        functools.partial(loss_kernel, len(earlier)),
        out_shape=(
            jax.ShapeDtypeStruct((count, width), F32),
            jax.ShapeDtypeStruct((3,), F32),
            jax.ShapeDtypeStruct((rows, width), BF16),
        ),
        in_specs=[SMEM] + [VMEM] * 4 + [SMEM] + [VMEM] * len(before),
        out_specs=(VMEM, SMEM, VMEM),
        scratch_shapes=[pltpu.VMEM((rows, width), BF16), pltpu.VMEM((3, 8, broad), F32)],
        input_output_aliases={4: 0},
        compiler_params=pltpu.CompilerParams(vmem_limit_bytes=VMEM_LIMIT),
        cost_estimate=cost(LOSS_FLOPS),
        name="loss_block",
    )(scal, image_unit, image, text, image_dunit, totals, *before)


def unit_kernel(half, scal, own, other, given, out):
    for rows in halves(own.shape[0])[half]:
        pair_grad = sigmoid_of(own[rows, :], other[...], scal[0], scal[1])
        out[rows, :] = given[rows, :] + weighted(pair_grad, other[...])


def raw_kernel(half, scal, own, raw, given, out, other):
    other[...] = unit_of(raw[...])
    unit_kernel(half, scal, own, other, given, out)


def halves(count):
    every = tiles(count)
    middle = len(every) // 2
    return every[:middle], every[middle:], every


def side_block(scal, own, other, raw, half, dunit):
    shapes = [jax.ShapeDtypeStruct(dunit.shape, F32)]
    if raw:
        shapes.append(jax.ShapeDtypeStruct(other.shape, BF16))
    return pl.pallas_call(
        functools.partial(raw_kernel if raw else unit_kernel, half),
        out_shape=shapes,
        in_specs=[SMEM] + [VMEM] * 3,
        out_specs=[VMEM] * len(shapes),
        input_output_aliases={3: 0},
        compiler_params=pltpu.CompilerParams(vmem_limit_bytes=VMEM_LIMIT),
        cost_estimate=cost(SIDE_FLOPS),
        name="side_block",
    )(scal, own, other, dunit)


def last_kernel(
    pair_count, scal, sums, image_own, text_own, image_unit, text_unit, image, text, image_in, text_in,
    image_grad, text_grad, loss, scalar_grads, other_image, other_text, image_out, text_out, sems,
):
    scale, bias = scal[0], scal[1]
    loss[0] = sums[0] * (1.0 / pair_count)
    scalar_grads[0] = scale * sums[1] * (1.0 / pair_count)
    scalar_grads[1] = sums[2] * (1.0 / pair_count)
    steps = image_own.shape[0] // LAST_TILE
    other_image[...] = unit_of(image[...])
    other_text[...] = unit_of(text[...])
    sides = (
        (image_own, image_unit, other_text, image_in, image_out, image_grad),
        (text_own, text_unit, other_image, text_in, text_out, text_grad),
    )
    copies = []
    for side, (own, unit, other, given, out, grad) in enumerate(sides):
        low = sigmoid_of(unit[...], other[...], scale, bias).astype(BF16)
        for step in range(steps):
            rows = slice(step * LAST_TILE, (step + 1) * LAST_TILE)
            dunit = given[rows, :] + jnp.dot(low[rows, :], other[...], preferred_element_type=F32)
            widened = own[rows, :].astype(F32)
            inverse = inverse_of(widened)
            along = jnp.sum(widened * dunit, axis=-1, keepdims=True) * inverse * inverse
            out[rows, :] = (dunit - widened * along) * (scale * inverse)
            copy = pltpu.make_async_copy(out.at[rows, :], grad.at[rows, :], sems.at[side, step])
            copy.start()
            copies.append(copy)
    for copy in copies:
        copy.wait()


def last_block(pair_count, scal, sums, image_own, text_own, image_unit, text_unit, image, text, image_dunit, text_dunit):
    count, width = image_own.shape
    rows = image.shape[0]
    grad = jax.ShapeDtypeStruct((count, width), F32)
    return pl.pallas_call(
        functools.partial(last_kernel, pair_count),
        out_shape=(grad, grad, jax.ShapeDtypeStruct((1,), F32), jax.ShapeDtypeStruct((2,), F32)),
        in_specs=[SMEM] * 2 + [VMEM] * 8,
        out_specs=(pl.BlockSpec(memory_space=pl.ANY), pl.BlockSpec(memory_space=pl.ANY), SMEM, SMEM),
        scratch_shapes=[
            pltpu.VMEM((rows, width), BF16),
            pltpu.VMEM((rows, width), BF16),
            pltpu.VMEM((count, width), F32),
            pltpu.VMEM((count, width), F32),
            pltpu.SemaphoreType.DMA((2, count // LAST_TILE)),
        ],
        compiler_params=pltpu.CompilerParams(vmem_limit_bytes=LAST_LIMIT),
        cost_estimate=cost(LAST_FLOPS),
        name="last_block",
    )(scal, sums, image_own, text_own, image_unit, text_unit, image, text, image_dunit, text_dunit)


def per_device(image_tower, text_tower, log_scale, bias):
    scal = jnp.concatenate([jnp.exp(log_scale), bias])
    back = functools.partial(passed_along, axis="blk", steps=-1)
    onward = functools.partial(passed_along, axis="blk", steps=1)
    first, second, third = slice(0, ENDS[0]), slice(ENDS[0], ENDS[1]), slice(ENDS[1], None)
    text_a, image_a = onward(text_tower[first]), back(image_tower[first])
    image_rest, text_rest = lax.optimization_barrier((image_tower, text_tower))
    text_b, image_b = onward(text_rest[second]), back(image_rest[second])
    image_unit, text_unit, image_dunit, text_dunit, totals = own_block(scal, image_tower, text_tower)
    image_rest, text_rest, image_dunit = lax.optimization_barrier((image_rest, text_rest, image_dunit))
    text_c, image_c = onward(text_rest[third]), back(image_rest[third])

    image_a, text_a, image_dunit = lax.optimization_barrier((image_a, text_a, image_dunit))
    far = [(back(image_a), onward(text_a))]
    image_dunit, text_dunit, totals, *units_a = piece_block(
        scal, image_unit, text_unit, image_a, text_a, image_dunit, text_dunit, totals, []
    )
    image_b, text_b, image_dunit = lax.optimization_barrier((image_b, text_b, image_dunit))
    far.append((back(image_b), onward(text_b)))
    image_dunit, text_dunit, totals, *units_b = piece_block(
        scal, image_unit, text_unit, image_b, text_b, image_dunit, text_dunit, totals, [units_a]
    )
    image_c, text_c, image_dunit = lax.optimization_barrier((image_c, text_c, image_dunit))
    rear = (image_c, text_c)
    image_dunit, totals, image_c = loss_block(
        scal, image_unit, image_c, text_c, image_dunit, totals, [units_a, units_b]
    )

    def first_half(own, raw):
        return lambda dunit: side_block(scal, own, raw, True, 0, dunit)

    def other_half(own, unit, half=1):
        return lambda dunit: side_block(scal, own, unit, False, half, dunit)

    (far_image, far_text), (near_image, near_text) = far
    totals = exchanged(totals, 0)
    totals, (text_dunit,) = beside(totals, 1, text_dunit, other_half(text_unit, image_c, 0))
    totals, (text_dunit,) = beside(totals, 2, text_dunit, other_half(text_unit, image_c))
    totals, rear = lax.optimization_barrier((totals, rear))
    rear = (back(rear[0]), onward(rear[1]))
    totals, (image_dunit, far_text) = beside(totals, 3, image_dunit, first_half(image_unit, far_text))
    totals, (image_dunit,) = beside(totals, 4, image_dunit, other_half(image_unit, far_text))
    totals, (text_dunit, far_image) = beside(totals, 5, text_dunit, first_half(text_unit, far_image))
    totals, (text_dunit,) = beside(totals, 6, text_dunit, other_half(text_unit, far_image))
    image_dunit, _ = side_block(scal, image_unit, near_text, True, 2, image_dunit)
    text_dunit, _ = side_block(scal, text_unit, near_image, True, 2, text_dunit)
    pair_count = text_tower.shape[0] * lax.axis_size("outer") * lax.axis_size("blk")
    image_grad, text_grad, loss, scalar_grads = last_block(
        pair_count, scal, totals, image_tower, text_tower, image_unit, text_unit, *rear, image_dunit, text_dunit
    )
    return (loss, image_grad, text_grad, scalar_grads)


def solution(mesh):
    return jax.shard_map(
        per_device,
        mesh=mesh,
        in_specs=(P(BOTH, None), P(BOTH, None), P(), P()),
        out_specs=(P(), P(BOTH, None), P(BOTH, None), P()),
        check_vma=False,
    )
```

```python
import functools

import functools

import jax
import jax.numpy as jnp
from jax import lax
from jax.experimental import pallas as pl
from jax.experimental.pallas import tpu as pltpu
from jax.sharding import PartitionSpec as P

F32 = jnp.float32
BF16 = jnp.bfloat16
TILE = 256
LAST_TILE = 128
ENDS = (512, 768)
OWN_FLOPS = 3_000_000_000
PIECE_FLOPS = 1_000
LOSS_FLOPS = 20_000_000_000
SIDE_FLOPS = 3_000_000_000
LAST_FLOPS = 3_000_000_000
EXCHANGES = (("outer", 1), ("outer", 2), ("blk", 4), ("blk", 8), ("blk", 16), ("blk", 2), ("blk", 1))
SMEM = pl.BlockSpec(memory_space=pltpu.SMEM)
VMEM = pl.BlockSpec(memory_space=pltpu.VMEM)
VMEM_LIMIT = 24 * 1024 * 1024
LAST_LIMIT = 30 * 1024 * 1024
BOTH = ("outer", "blk")


def passed_along(value, axis, steps):
    count = lax.axis_size(axis)
    pairs = [(source, (source + steps) % count) for source in range(count)]
    return lax.ppermute(value, axis, pairs)


def exchanged(totals, step):
    axis, bit = EXCHANGES[step]
    pairs = [(source, source ^ bit) for source in range(lax.axis_size(axis))]
    return totals + lax.ppermute(totals, axis, pairs)


def beside(totals, step, dunit, work):
    totals, dunit = lax.optimization_barrier((totals, dunit))
    return lax.optimization_barrier((exchanged(totals, step), work(dunit)))


def cost(flops):
    return pl.CostEstimate(flops=flops, bytes_accessed=1_000_000, transcendentals=0)


def inverse_of(widened):
    return lax.rsqrt(jnp.sum(widened * widened, axis=-1, keepdims=True) + 1e-06)


def unit_of(tower):
    widened = tower.astype(F32)
    return (widened * inverse_of(widened)).astype(BF16)


def products(rows, others):
    return lax.dot_general(rows, others, (((1,), (1,)), ((), ())), preferred_element_type=F32)


def weighted(pair_grad, others):
    return jnp.dot(pair_grad.astype(BF16), others, preferred_element_type=F32)


def sigmoid_of(rows, others, scale, bias):
    return pl.reciprocal(1.0 + jnp.exp(-scale * products(rows, others) - bias))


def folded(values):
    return jnp.sum(values.reshape(values.shape[0] // 8, 8, values.shape[1]), axis=0)


def scored(sums, rows, others, scale, bias):
    cosine = products(rows, others)
    exped = jnp.exp(scale * cosine + bias)
    above = 1.0 + exped
    inverse = pl.reciprocal(above)
    pair_grad = exped * inverse
    width = others.shape[0]
    sums[0, :, :width] += folded(jnp.log(above) + (exped - (above - 1.0)) * inverse)
    sums[1, :, :width] += folded(pair_grad * cosine)
    sums[2, :, :width] += folded(pair_grad)
    return pair_grad


def tile_at(step):
    return pl.ds(pl.multiple_of(step * TILE, TILE), TILE)


def own_kernel(scal, image, text, image_unit, text_unit, image_dunit, text_dunit, totals, sums, grads):
    scale, bias = scal[0], scal[1]
    steps = image.shape[0] // TILE
    sums[...] = jnp.zeros_like(sums)

    @pl.loop(0, steps)
    def _(t):
        rows = tile_at(t)
        image_unit[rows, :] = unit_of(image[rows, :])
        text_unit[rows, :] = unit_of(text[rows, :])

    @pl.loop(0, steps)
    def _(t):
        rows = tile_at(t)
        cosine = products(image_unit[rows, :], text_unit[...])
        logit = scale * cosine + bias
        exped = jnp.exp(logit)
        pair_grad = exped / (1.0 + exped)
        diagonal = (
            lax.broadcasted_iota(jnp.int32, cosine.shape, 0) + t * TILE
            == lax.broadcasted_iota(jnp.int32, cosine.shape, 1)
        )
        pair_grad = jnp.where(diagonal, pair_grad - 1.0, pair_grad)
        sums[0] += folded(jnp.log1p(exped) - jnp.where(diagonal, logit, 0.0))
        sums[1] += folded(pair_grad * cosine)
        sums[2] += folded(pair_grad)
        grads[rows, :] = pair_grad.astype(BF16)
        image_dunit[rows, :] = weighted(pair_grad, text_unit[...])

    @pl.loop(0, steps)
    def _(t):
        rows = tile_at(t)
        text_dunit[rows, :] = lax.dot_general(
            grads[:, rows], image_unit[...], (((0,), (0,)), ((), ())), preferred_element_type=F32
        )

    for kind in range(3):
        totals[kind] = jnp.sum(sums[kind])


def own_block(scal, image, text):
    count, width = image.shape
    tower = jax.ShapeDtypeStruct((count, width), BF16)
    dunit = jax.ShapeDtypeStruct((count, width), F32)
    return pl.pallas_call(
        own_kernel,
        out_shape=(tower, tower, dunit, dunit, jax.ShapeDtypeStruct((3,), F32)),
        in_specs=[SMEM, VMEM, VMEM],
        out_specs=(VMEM, VMEM, VMEM, VMEM, SMEM),
        scratch_shapes=[pltpu.VMEM((3, 8, count), F32), pltpu.VMEM((count, count), BF16)],
        compiler_params=pltpu.CompilerParams(vmem_limit_bytes=VMEM_LIMIT),
        cost_estimate=cost(OWN_FLOPS),
        name="own_block",
    )(scal, image, text)


def tiles(count):
    return [slice(start, start + TILE) for start in range(0, count, TILE)]


def cross_scored(sums, other_image, other_text, image_before, text_before, scale, bias):
    for rows in tiles(other_image.shape[0]):
        for text_units in (other_text, *text_before):
            scored(sums, other_image[rows, :], text_units[...], scale, bias)
    for image_units in image_before:
        for rows in tiles(image_units.shape[0]):
            scored(sums, image_units[rows, :], other_text[...], scale, bias)


def piece_kernel(before, scal, image_unit, text_unit, image, text, image_in, text_in, totals_in, *rest):
    image_before, text_before = rest[:before], rest[before : 2 * before]
    image_dunit, text_dunit, totals, other_image, other_text, sums = rest[2 * before :]
    scale, bias = scal[0], scal[1]
    other_image[...] = unit_of(image[...])
    other_text[...] = unit_of(text[...])
    sums[...] = jnp.zeros_like(sums)
    for rows in tiles(image_unit.shape[0]):
        pair_grad = scored(sums, image_unit[rows, :], other_text[...], scale, bias)
        image_dunit[rows, :] = image_in[rows, :] + weighted(pair_grad, other_text[...])
        pair_grad = sigmoid_of(text_unit[rows, :], other_image[...], scale, bias)
        text_dunit[rows, :] = text_in[rows, :] + weighted(pair_grad, other_image[...])
    cross_scored(sums, other_image, other_text, image_before, text_before, scale, bias)
    for kind in range(3):
        totals[kind] = totals_in[kind] + jnp.sum(sums[kind])


def piece_block(scal, image_unit, text_unit, image, text, image_dunit, text_dunit, totals, earlier):
    count, width = image_unit.shape
    rows = image.shape[0]
    dunit = jax.ShapeDtypeStruct((count, width), F32)
    unit = jax.ShapeDtypeStruct((rows, width), BF16)
    before = [pair[side] for side in (0, 1) for pair in earlier]
    broad = max(piece.shape[0] for piece in [image, *before])
    return pl.pallas_call(
        functools.partial(piece_kernel, len(earlier)),
        out_shape=(dunit, dunit, jax.ShapeDtypeStruct((3,), F32), unit, unit),
        in_specs=[SMEM] + [VMEM] * 6 + [SMEM] + [VMEM] * len(before),
        out_specs=(VMEM, VMEM, SMEM, VMEM, VMEM),
        scratch_shapes=[pltpu.VMEM((3, 8, broad), F32)],
        input_output_aliases={5: 0, 6: 1},
        compiler_params=pltpu.CompilerParams(vmem_limit_bytes=VMEM_LIMIT),
        cost_estimate=cost(PIECE_FLOPS),
        name="piece_block",
    )(scal, image_unit, text_unit, image, text, image_dunit, text_dunit, totals, *before)


def loss_kernel(before, scal, image_unit, image, text, image_in, totals_in, *rest):
    image_before, text_before = rest[:before], rest[before : 2 * before]
    image_dunit, totals, other_image, other_text, sums = rest[2 * before :]
    scale, bias = scal[0], scal[1]
    other_image[...] = unit_of(image[...])
    other_text[...] = unit_of(text[...])
    sums[...] = jnp.zeros_like(sums)
    for rows in tiles(image_unit.shape[0]):
        pair_grad = scored(sums, image_unit[rows, :], other_text[...], scale, bias)
        image_dunit[rows, :] = image_in[rows, :] + weighted(pair_grad, other_text[...])
    cross_scored(sums, other_image, other_text, image_before, text_before, scale, bias)
    for kind in range(3):
        totals[kind] = totals_in[kind] + jnp.sum(sums[kind])


def loss_block(scal, image_unit, image, text, image_dunit, totals, earlier):
    count, width = image_unit.shape
    rows = image.shape[0]
    before = [pair[side] for side in (0, 1) for pair in earlier]
    broad = max(piece.shape[0] for piece in [image, *before])
    return pl.pallas_call(
        functools.partial(loss_kernel, len(earlier)),
        out_shape=(
            jax.ShapeDtypeStruct((count, width), F32),
            jax.ShapeDtypeStruct((3,), F32),
            jax.ShapeDtypeStruct((rows, width), BF16),
        ),
        in_specs=[SMEM] + [VMEM] * 4 + [SMEM] + [VMEM] * len(before),
        out_specs=(VMEM, SMEM, VMEM),
        scratch_shapes=[pltpu.VMEM((rows, width), BF16), pltpu.VMEM((3, 8, broad), F32)],
        input_output_aliases={4: 0},
        compiler_params=pltpu.CompilerParams(vmem_limit_bytes=VMEM_LIMIT),
        cost_estimate=cost(LOSS_FLOPS),
        name="loss_block",
    )(scal, image_unit, image, text, image_dunit, totals, *before)


def unit_kernel(half, scal, own, other, given, out):
    for rows in halves(own.shape[0])[half]:
        pair_grad = sigmoid_of(own[rows, :], other[...], scal[0], scal[1])
        out[rows, :] = given[rows, :] + weighted(pair_grad, other[...])


def raw_kernel(half, scal, own, raw, given, out, other):
    other[...] = unit_of(raw[...])
    unit_kernel(half, scal, own, other, given, out)


def halves(count):
    every = tiles(count)
    middle = len(every) // 2
    return every[:middle], every[middle:], every


def side_block(scal, own, other, raw, half, dunit):
    shapes = [jax.ShapeDtypeStruct(dunit.shape, F32)]
    if raw:
        shapes.append(jax.ShapeDtypeStruct(other.shape, BF16))
    return pl.pallas_call(
        functools.partial(raw_kernel if raw else unit_kernel, half),
        out_shape=shapes,
        in_specs=[SMEM] + [VMEM] * 3,
        out_specs=[VMEM] * len(shapes),
        input_output_aliases={3: 0},
        compiler_params=pltpu.CompilerParams(vmem_limit_bytes=VMEM_LIMIT),
        cost_estimate=cost(SIDE_FLOPS),
        name="side_block",
    )(scal, own, other, dunit)


def last_kernel(
    scal, image_own, text_own, image_unit, text_unit, image, text, image_in, text_in,
    image_grad, text_grad, other_image, other_text, image_out, text_out, sems,
):
    scale, bias = scal[0], scal[1]
    steps = image_own.shape[0] // LAST_TILE
    other_image[...] = unit_of(image[...])
    other_text[...] = unit_of(text[...])
    sides = (
        (image_own, image_unit, other_text, image_in, image_out, image_grad),
        (text_own, text_unit, other_image, text_in, text_out, text_grad),
    )
    copies = []
    for side, (own, unit, other, given, out, grad) in enumerate(sides):
        low = sigmoid_of(unit[...], other[...], scale, bias).astype(BF16)
        for step in range(steps):
            rows = slice(step * LAST_TILE, (step + 1) * LAST_TILE)
            dunit = given[rows, :] + jnp.dot(low[rows, :], other[...], preferred_element_type=F32)
            widened = own[rows, :].astype(F32)
            inverse = inverse_of(widened)
            along = jnp.sum(widened * dunit, axis=-1, keepdims=True) * inverse * inverse
            out[rows, :] = (dunit - widened * along) * (scale * inverse)
            copy = pltpu.make_async_copy(out.at[rows, :], grad.at[rows, :], sems.at[side, step])
            copy.start()
            copies.append(copy)
    for copy in copies:
        copy.wait()


def last_block(scal, image_own, text_own, image_unit, text_unit, image, text, image_dunit, text_dunit):
    count, width = image_own.shape
    rows = image.shape[0]
    grad = jax.ShapeDtypeStruct((count, width), F32)
    return pl.pallas_call(
        last_kernel,
        out_shape=(grad, grad),
        in_specs=[SMEM] + [VMEM] * 8,
        out_specs=(pl.BlockSpec(memory_space=pl.ANY), pl.BlockSpec(memory_space=pl.ANY)),
        scratch_shapes=[
            pltpu.VMEM((rows, width), BF16),
            pltpu.VMEM((rows, width), BF16),
            pltpu.VMEM((count, width), F32),
            pltpu.VMEM((count, width), F32),
            pltpu.SemaphoreType.DMA((2, count // LAST_TILE)),
        ],
        compiler_params=pltpu.CompilerParams(vmem_limit_bytes=LAST_LIMIT),
        cost_estimate=cost(LAST_FLOPS),
        name="last_block",
    )(scal, image_own, text_own, image_unit, text_unit, image, text, image_dunit, text_dunit)


def per_device(image_tower, text_tower, log_scale, bias):
    scal = jnp.concatenate([jnp.exp(log_scale), bias])
    back = functools.partial(passed_along, axis="blk", steps=-1)
    onward = functools.partial(passed_along, axis="blk", steps=1)
    first, second, third = slice(0, ENDS[0]), slice(ENDS[0], ENDS[1]), slice(ENDS[1], None)
    text_a, image_a = onward(text_tower[first]), back(image_tower[first])
    image_rest, text_rest = lax.optimization_barrier((image_tower, text_tower))
    text_b, image_b = onward(text_rest[second]), back(image_rest[second])
    image_unit, text_unit, image_dunit, text_dunit, totals = own_block(scal, image_tower, text_tower)
    image_rest, text_rest, image_dunit = lax.optimization_barrier((image_rest, text_rest, image_dunit))
    text_c, image_c = onward(text_rest[third]), back(image_rest[third])

    image_a, text_a, image_dunit = lax.optimization_barrier((image_a, text_a, image_dunit))
    far = [(back(image_a), onward(text_a))]
    image_dunit, text_dunit, totals, *units_a = piece_block(
        scal, image_unit, text_unit, image_a, text_a, image_dunit, text_dunit, totals, []
    )
    image_b, text_b, image_dunit = lax.optimization_barrier((image_b, text_b, image_dunit))
    far.append((back(image_b), onward(text_b)))
    image_dunit, text_dunit, totals, *units_b = piece_block(
        scal, image_unit, text_unit, image_b, text_b, image_dunit, text_dunit, totals, [units_a]
    )
    image_c, text_c, image_dunit = lax.optimization_barrier((image_c, text_c, image_dunit))
    rear = (image_c, text_c)
    image_dunit, totals, image_c = loss_block(
        scal, image_unit, image_c, text_c, image_dunit, totals, [units_a, units_b]
    )

    def first_half(own, raw):
        return lambda dunit: side_block(scal, own, raw, True, 0, dunit)

    def other_half(own, unit, half=1):
        return lambda dunit: side_block(scal, own, unit, False, half, dunit)

    (far_image, far_text), (near_image, near_text) = far
    totals, (text_dunit,) = beside(totals, 0, text_dunit, other_half(text_unit, image_c, 0))
    totals, (text_dunit,) = beside(totals, 1, text_dunit, other_half(text_unit, image_c))
    totals = exchanged(totals, 2)
    totals, rear, far_image, far_text = lax.optimization_barrier((totals, rear, far_image, far_text))
    rear = (back(rear[0]), onward(rear[1]))
    totals, (image_dunit, far_text) = beside(totals, 3, image_dunit, first_half(image_unit, far_text))
    totals, (image_dunit,) = beside(totals, 4, image_dunit, other_half(image_unit, far_text))
    totals, (text_dunit, far_image) = beside(totals, 5, text_dunit, first_half(text_unit, far_image))
    totals, (text_dunit,) = beside(totals, 6, text_dunit, other_half(text_unit, far_image))
    image_dunit, _ = side_block(scal, image_unit, near_text, True, 2, image_dunit)
    text_dunit, _ = side_block(scal, text_unit, near_image, True, 2, text_dunit)
    pair_count = text_tower.shape[0] * lax.axis_size("outer") * lax.axis_size("blk")
    means = totals * jnp.stack([jnp.float32(1.0), scal[0], jnp.float32(1.0)]) / pair_count
    loss, scalar_grads = means[:1], means[1:]
    image_grad, text_grad = last_block(
        scal, image_tower, text_tower, image_unit, text_unit, *rear, image_dunit, text_dunit
    )
    return (loss, image_grad, text_grad, scalar_grads)


def solution(mesh):
    return jax.shard_map(
        per_device,
        mesh=mesh,
        in_specs=(P(BOTH, None), P(BOTH, None), P(), P()),
        out_specs=(P(), P(BOTH, None), P(BOTH, None), P()),
        check_vma=False,
    )
```

```python
import functools

import functools

import jax
import jax.numpy as jnp
from jax import lax
from jax.experimental import pallas as pl
from jax.experimental.pallas import tpu as pltpu
from jax.sharding import PartitionSpec as P

F32 = jnp.float32
BF16 = jnp.bfloat16
TILE = 256
LAST_TILE = 128
ENDS = (512, 768)
OWN_FLOPS = 3_000_000_000
PIECE_FLOPS = 1_000
LOSS_FLOPS = 20_000_000_000
SIDE_FLOPS = 3_000_000_000
LAST_FLOPS = 3_000_000_000
EXCHANGES = (("outer", 1), ("outer", 2), ("blk", 4), ("blk", 8), ("blk", 16), ("blk", 2), ("blk", 1))
SMEM = pl.BlockSpec(memory_space=pltpu.SMEM)
VMEM = pl.BlockSpec(memory_space=pltpu.VMEM)
VMEM_LIMIT = 24 * 1024 * 1024
LAST_LIMIT = 30 * 1024 * 1024
BOTH = ("outer", "blk")


def passed_along(value, axis, steps):
    count = lax.axis_size(axis)
    pairs = [(source, (source + steps) % count) for source in range(count)]
    return lax.ppermute(value, axis, pairs)


def exchanged(totals, step):
    axis, bit = EXCHANGES[step]
    pairs = [(source, source ^ bit) for source in range(lax.axis_size(axis))]
    return totals + lax.ppermute(totals, axis, pairs)


def beside(totals, step, dunit, work):
    totals, dunit = lax.optimization_barrier((totals, dunit))
    return lax.optimization_barrier((exchanged(totals, step), work(dunit)))


def cost(flops):
    return pl.CostEstimate(flops=flops, bytes_accessed=1_000_000, transcendentals=0)


def inverse_of(widened):
    return lax.rsqrt(jnp.sum(widened * widened, axis=-1, keepdims=True) + 1e-06)


def unit_of(tower):
    widened = tower.astype(F32)
    return (widened * inverse_of(widened)).astype(BF16)


def products(rows, others):
    return lax.dot_general(rows, others, (((1,), (1,)), ((), ())), preferred_element_type=F32)


def weighted(pair_grad, others):
    return jnp.dot(pair_grad.astype(BF16), others, preferred_element_type=F32)


def sigmoid_of(rows, others, scale, bias):
    return pl.reciprocal(1.0 + jnp.exp(-scale * products(rows, others) - bias))


def folded(values):
    return jnp.sum(values.reshape(values.shape[0] // 8, 8, values.shape[1]), axis=0)


def scored(sums, rows, others, scale, bias):
    cosine = products(rows, others)
    exped = jnp.exp(scale * cosine + bias)
    above = 1.0 + exped
    inverse = pl.reciprocal(above)
    pair_grad = exped * inverse
    width = others.shape[0]
    sums[0, :, :width] += folded(jnp.log(above) + (exped - (above - 1.0)) * inverse)
    sums[1, :, :width] += folded(pair_grad * cosine)
    sums[2, :, :width] += folded(pair_grad)
    return pair_grad


def tile_at(step):
    return pl.ds(pl.multiple_of(step * TILE, TILE), TILE)


def own_kernel(scal, image, text, image_unit, text_unit, image_dunit, text_dunit, totals, sums, grads):
    scale, bias = scal[0], scal[1]
    steps = image.shape[0] // TILE
    sums[...] = jnp.zeros_like(sums)

    @pl.loop(0, steps)
    def _(t):
        rows = tile_at(t)
        image_unit[rows, :] = unit_of(image[rows, :])
        text_unit[rows, :] = unit_of(text[rows, :])

    @pl.loop(0, steps)
    def _(t):
        rows = tile_at(t)
        cosine = products(image_unit[rows, :], text_unit[...])
        logit = scale * cosine + bias
        exped = jnp.exp(logit)
        pair_grad = exped / (1.0 + exped)
        diagonal = (
            lax.broadcasted_iota(jnp.int32, cosine.shape, 0) + t * TILE
            == lax.broadcasted_iota(jnp.int32, cosine.shape, 1)
        )
        pair_grad = jnp.where(diagonal, pair_grad - 1.0, pair_grad)
        sums[0] += folded(jnp.log1p(exped) - jnp.where(diagonal, logit, 0.0))
        sums[1] += folded(pair_grad * cosine)
        sums[2] += folded(pair_grad)
        grads[rows, :] = pair_grad.astype(BF16)
        image_dunit[rows, :] = weighted(pair_grad, text_unit[...])

    @pl.loop(0, steps)
    def _(t):
        rows = tile_at(t)
        text_dunit[rows, :] = lax.dot_general(
            grads[:, rows], image_unit[...], (((0,), (0,)), ((), ())), preferred_element_type=F32
        )

    for kind in range(3):
        totals[kind] = jnp.sum(sums[kind])


def own_block(scal, image, text):
    count, width = image.shape
    tower = jax.ShapeDtypeStruct((count, width), BF16)
    dunit = jax.ShapeDtypeStruct((count, width), F32)
    return pl.pallas_call(
        own_kernel,
        out_shape=(tower, tower, dunit, dunit, jax.ShapeDtypeStruct((3,), F32)),
        in_specs=[SMEM, VMEM, VMEM],
        out_specs=(VMEM, VMEM, VMEM, VMEM, SMEM),
        scratch_shapes=[pltpu.VMEM((3, 8, count), F32), pltpu.VMEM((count, count), BF16)],
        compiler_params=pltpu.CompilerParams(vmem_limit_bytes=VMEM_LIMIT),
        cost_estimate=cost(OWN_FLOPS),
        name="own_block",
    )(scal, image, text)


def tiles(count):
    return [slice(start, start + TILE) for start in range(0, count, TILE)]


def cross_scored(sums, other_image, other_text, image_before, text_before, scale, bias):
    for rows in tiles(other_image.shape[0]):
        for text_units in (other_text, *text_before):
            scored(sums, other_image[rows, :], text_units[...], scale, bias)
    for image_units in image_before:
        for rows in tiles(image_units.shape[0]):
            scored(sums, image_units[rows, :], other_text[...], scale, bias)


def piece_kernel(before, scal, image_unit, text_unit, image, text, image_in, text_in, totals_in, *rest):
    image_before, text_before = rest[:before], rest[before : 2 * before]
    image_dunit, text_dunit, totals, other_image, other_text, sums = rest[2 * before :]
    scale, bias = scal[0], scal[1]
    other_image[...] = unit_of(image[...])
    other_text[...] = unit_of(text[...])
    sums[...] = jnp.zeros_like(sums)
    for rows in tiles(image_unit.shape[0]):
        pair_grad = scored(sums, image_unit[rows, :], other_text[...], scale, bias)
        image_dunit[rows, :] = image_in[rows, :] + weighted(pair_grad, other_text[...])
        pair_grad = sigmoid_of(text_unit[rows, :], other_image[...], scale, bias)
        text_dunit[rows, :] = text_in[rows, :] + weighted(pair_grad, other_image[...])
    cross_scored(sums, other_image, other_text, image_before, text_before, scale, bias)
    for kind in range(3):
        totals[kind] = totals_in[kind] + jnp.sum(sums[kind])


def piece_block(scal, image_unit, text_unit, image, text, image_dunit, text_dunit, totals, earlier):
    count, width = image_unit.shape
    rows = image.shape[0]
    dunit = jax.ShapeDtypeStruct((count, width), F32)
    unit = jax.ShapeDtypeStruct((rows, width), BF16)
    before = [pair[side] for side in (0, 1) for pair in earlier]
    broad = max(piece.shape[0] for piece in [image, *before])
    return pl.pallas_call(
        functools.partial(piece_kernel, len(earlier)),
        out_shape=(dunit, dunit, jax.ShapeDtypeStruct((3,), F32), unit, unit),
        in_specs=[SMEM] + [VMEM] * 6 + [SMEM] + [VMEM] * len(before),
        out_specs=(VMEM, VMEM, SMEM, VMEM, VMEM),
        scratch_shapes=[pltpu.VMEM((3, 8, broad), F32)],
        input_output_aliases={5: 0, 6: 1},
        compiler_params=pltpu.CompilerParams(vmem_limit_bytes=VMEM_LIMIT),
        cost_estimate=cost(PIECE_FLOPS),
        name="piece_block",
    )(scal, image_unit, text_unit, image, text, image_dunit, text_dunit, totals, *before)


def loss_kernel(before, scal, image_unit, image, text, image_in, totals_in, *rest):
    image_before, text_before = rest[:before], rest[before : 2 * before]
    image_dunit, totals, other_image, other_text, sums = rest[2 * before :]
    scale, bias = scal[0], scal[1]
    other_image[...] = unit_of(image[...])
    other_text[...] = unit_of(text[...])
    sums[...] = jnp.zeros_like(sums)
    for rows in tiles(image_unit.shape[0]):
        pair_grad = scored(sums, image_unit[rows, :], other_text[...], scale, bias)
        image_dunit[rows, :] = image_in[rows, :] + weighted(pair_grad, other_text[...])
    cross_scored(sums, other_image, other_text, image_before, text_before, scale, bias)
    for kind in range(3):
        totals[kind] = totals_in[kind] + jnp.sum(sums[kind])


def loss_block(scal, image_unit, image, text, image_dunit, totals, earlier):
    count, width = image_unit.shape
    rows = image.shape[0]
    before = [pair[side] for side in (0, 1) for pair in earlier]
    broad = max(piece.shape[0] for piece in [image, *before])
    return pl.pallas_call(
        functools.partial(loss_kernel, len(earlier)),
        out_shape=(
            jax.ShapeDtypeStruct((count, width), F32),
            jax.ShapeDtypeStruct((3,), F32),
            jax.ShapeDtypeStruct((rows, width), BF16),
        ),
        in_specs=[SMEM] + [VMEM] * 4 + [SMEM] + [VMEM] * len(before),
        out_specs=(VMEM, SMEM, VMEM),
        scratch_shapes=[pltpu.VMEM((rows, width), BF16), pltpu.VMEM((3, 8, broad), F32)],
        input_output_aliases={4: 0},
        compiler_params=pltpu.CompilerParams(vmem_limit_bytes=VMEM_LIMIT),
        cost_estimate=cost(LOSS_FLOPS),
        name="loss_block",
    )(scal, image_unit, image, text, image_dunit, totals, *before)


def unit_kernel(half, scal, own, other, given, out):
    for rows in halves(own.shape[0])[half]:
        pair_grad = sigmoid_of(own[rows, :], other[...], scal[0], scal[1])
        out[rows, :] = given[rows, :] + weighted(pair_grad, other[...])


def raw_kernel(half, scal, own, raw, given, out, other):
    other[...] = unit_of(raw[...])
    unit_kernel(half, scal, own, other, given, out)


def halves(count):
    every = tiles(count)
    middle = len(every) // 2
    return every[:middle], every[middle:], every


def side_block(scal, own, other, raw, half, dunit):
    shapes = [jax.ShapeDtypeStruct(dunit.shape, F32)]
    if raw:
        shapes.append(jax.ShapeDtypeStruct(other.shape, BF16))
    return pl.pallas_call(
        functools.partial(raw_kernel if raw else unit_kernel, half),
        out_shape=shapes,
        in_specs=[SMEM] + [VMEM] * 3,
        out_specs=[VMEM] * len(shapes),
        input_output_aliases={3: 0},
        compiler_params=pltpu.CompilerParams(vmem_limit_bytes=VMEM_LIMIT),
        cost_estimate=cost(SIDE_FLOPS),
        name="side_block",
    )(scal, own, other, dunit)


def last_kernel(
    scal, image_own, text_own, image_unit, text_unit, image, text, image_in, text_in,
    image_grad, text_grad, other_image, other_text, image_out, text_out, sems,
):
    scale, bias = scal[0], scal[1]
    steps = image_own.shape[0] // LAST_TILE
    other_image[...] = unit_of(image[...])
    other_text[...] = unit_of(text[...])
    sides = (
        (image_own, image_unit, other_text, image_in, image_out, image_grad),
        (text_own, text_unit, other_image, text_in, text_out, text_grad),
    )
    copies = []
    for side, (own, unit, other, given, out, grad) in enumerate(sides):
        low = sigmoid_of(unit[...], other[...], scale, bias).astype(BF16)
        for step in range(steps):
            rows = slice(step * LAST_TILE, (step + 1) * LAST_TILE)
            dunit = given[rows, :] + jnp.dot(low[rows, :], other[...], preferred_element_type=F32)
            widened = own[rows, :].astype(F32)
            inverse = inverse_of(widened)
            along = jnp.sum(widened * dunit, axis=-1, keepdims=True) * inverse * inverse
            out[rows, :] = (dunit - widened * along) * (scale * inverse)
            copy = pltpu.make_async_copy(out.at[rows, :], grad.at[rows, :], sems.at[side, step])
            copy.start()
            copies.append(copy)
    for copy in copies:
        copy.wait()


def last_block(scal, image_own, text_own, image_unit, text_unit, image, text, image_dunit, text_dunit):
    count, width = image_own.shape
    rows = image.shape[0]
    grad = jax.ShapeDtypeStruct((count, width), F32)
    return pl.pallas_call(
        last_kernel,
        out_shape=(grad, grad),
        in_specs=[SMEM] + [VMEM] * 8,
        out_specs=(pl.BlockSpec(memory_space=pl.ANY), pl.BlockSpec(memory_space=pl.ANY)),
        scratch_shapes=[
            pltpu.VMEM((rows, width), BF16),
            pltpu.VMEM((rows, width), BF16),
            pltpu.VMEM((count, width), F32),
            pltpu.VMEM((count, width), F32),
            pltpu.SemaphoreType.DMA((2, count // LAST_TILE)),
        ],
        compiler_params=pltpu.CompilerParams(vmem_limit_bytes=LAST_LIMIT),
        cost_estimate=cost(LAST_FLOPS),
        name="last_block",
    )(scal, image_own, text_own, image_unit, text_unit, image, text, image_dunit, text_dunit)


def per_device(image_tower, text_tower, log_scale, bias):
    scal = jnp.concatenate([jnp.exp(log_scale), bias])
    back = functools.partial(passed_along, axis="blk", steps=-1)
    onward = functools.partial(passed_along, axis="blk", steps=1)
    first, second, third = slice(0, ENDS[0]), slice(ENDS[0], ENDS[1]), slice(ENDS[1], None)
    text_a, image_a = onward(text_tower[first]), back(image_tower[first])
    image_rest, text_rest = lax.optimization_barrier((image_tower, text_tower))
    text_b, image_b = onward(text_rest[second]), back(image_rest[second])
    image_unit, text_unit, image_dunit, text_dunit, totals = own_block(scal, image_tower, text_tower)
    image_rest, text_rest, image_dunit = lax.optimization_barrier((image_rest, text_rest, image_dunit))
    text_c, image_c = onward(text_rest[third]), back(image_rest[third])

    image_a, text_a, image_dunit = lax.optimization_barrier((image_a, text_a, image_dunit))
    far = [(back(image_a), onward(text_a))]
    image_dunit, text_dunit, totals, *units_a = piece_block(
        scal, image_unit, text_unit, image_a, text_a, image_dunit, text_dunit, totals, []
    )
    image_b, text_b, image_dunit = lax.optimization_barrier((image_b, text_b, image_dunit))
    far.append((back(image_b), onward(text_b)))
    image_dunit, text_dunit, totals, *units_b = piece_block(
        scal, image_unit, text_unit, image_b, text_b, image_dunit, text_dunit, totals, [units_a]
    )
    image_c, text_c, image_dunit = lax.optimization_barrier((image_c, text_c, image_dunit))
    rear = (image_c, text_c)
    image_dunit, totals, image_c = loss_block(
        scal, image_unit, image_c, text_c, image_dunit, totals, [units_a, units_b]
    )

    def first_half(own, raw):
        return lambda dunit: side_block(scal, own, raw, True, 0, dunit)

    def other_half(own, unit, half=1):
        return lambda dunit: side_block(scal, own, unit, False, half, dunit)

    (far_image, far_text), (near_image, near_text) = far
    totals, (text_dunit,) = beside(totals, 0, text_dunit, other_half(text_unit, image_c, 0))
    totals, (text_dunit,) = beside(totals, 1, text_dunit, other_half(text_unit, image_c))
    totals = exchanged(totals, 2)
    totals = exchanged(totals, 3)
    totals, rear, far_image, far_text = lax.optimization_barrier((totals, rear, far_image, far_text))
    rear = (back(rear[0]), onward(rear[1]))
    totals, (image_dunit, far_text) = beside(totals, 4, image_dunit, first_half(image_unit, far_text))
    totals, (image_dunit,) = beside(totals, 5, image_dunit, other_half(image_unit, far_text))
    totals, (text_dunit, far_image) = beside(totals, 6, text_dunit, first_half(text_unit, far_image))
    text_dunit, = other_half(text_unit, far_image)(text_dunit)
    image_dunit, _ = side_block(scal, image_unit, near_text, True, 2, image_dunit)
    text_dunit, _ = side_block(scal, text_unit, near_image, True, 2, text_dunit)
    pair_count = text_tower.shape[0] * lax.axis_size("outer") * lax.axis_size("blk")
    means = totals * jnp.stack([jnp.float32(1.0), scal[0], jnp.float32(1.0)]) / pair_count
    loss, scalar_grads = means[:1], means[1:]
    image_grad, text_grad = last_block(
        scal, image_tower, text_tower, image_unit, text_unit, *rear, image_dunit, text_dunit
    )
    return (loss, image_grad, text_grad, scalar_grads)


def solution(mesh):
    return jax.shard_map(
        per_device,
        mesh=mesh,
        in_specs=(P(BOTH, None), P(BOTH, None), P(), P()),
        out_specs=(P(), P(BOTH, None), P(BOTH, None), P()),
        check_vma=False,
    )
```

```python
import functools

import functools

import jax
import jax.numpy as jnp
from jax import lax
from jax.experimental import pallas as pl
from jax.experimental.pallas import tpu as pltpu
from jax.sharding import PartitionSpec as P

F32 = jnp.float32
BF16 = jnp.bfloat16
TILE = 256
LAST_TILE = 128
ENDS = (512, 768)
OWN_FLOPS = 3_000_000_000
PIECE_FLOPS = 1_000
LOSS_FLOPS = 20_000_000_000
SIDE_FLOPS = 3_000_000_000
LAST_FLOPS = 3_000_000_000
EXCHANGES = (("outer", 1), ("outer", 2), ("blk", 4), ("blk", 8), ("blk", 16), ("blk", 2), ("blk", 1))
SMEM = pl.BlockSpec(memory_space=pltpu.SMEM)
VMEM = pl.BlockSpec(memory_space=pltpu.VMEM)
VMEM_LIMIT = 24 * 1024 * 1024
LAST_LIMIT = 30 * 1024 * 1024
BOTH = ("outer", "blk")


def passed_along(value, axis, steps):
    count = lax.axis_size(axis)
    pairs = [(source, (source + steps) % count) for source in range(count)]
    return lax.ppermute(value, axis, pairs)


def exchanged(totals, step):
    axis, bit = EXCHANGES[step]
    pairs = [(source, source ^ bit) for source in range(lax.axis_size(axis))]
    return totals + lax.ppermute(totals, axis, pairs)


def beside(totals, step, dunit, work):
    totals, dunit = lax.optimization_barrier((totals, dunit))
    return lax.optimization_barrier((exchanged(totals, step), work(dunit)))


def cost(flops):
    return pl.CostEstimate(flops=flops, bytes_accessed=1_000_000, transcendentals=0)


def inverse_of(widened):
    return lax.rsqrt(jnp.sum(widened * widened, axis=-1, keepdims=True) + 1e-06)


def unit_of(tower):
    widened = tower.astype(F32)
    return (widened * inverse_of(widened)).astype(BF16)


def products(rows, others):
    return lax.dot_general(rows, others, (((1,), (1,)), ((), ())), preferred_element_type=F32)


def weighted(pair_grad, others):
    return jnp.dot(pair_grad.astype(BF16), others, preferred_element_type=F32)


def sigmoid_of(rows, others, scale, bias):
    return pl.reciprocal(1.0 + jnp.exp(-scale * products(rows, others) - bias))


def folded(values):
    return jnp.sum(values.reshape(values.shape[0] // 8, 8, values.shape[1]), axis=0)


def scored(sums, rows, others, scale, bias):
    cosine = products(rows, others)
    exped = jnp.exp(scale * cosine + bias)
    above = 1.0 + exped
    inverse = pl.reciprocal(above)
    pair_grad = exped * inverse
    width = others.shape[0]
    sums[0, :, :width] += folded(jnp.log(above) + (exped - (above - 1.0)) * inverse)
    sums[1, :, :width] += folded(pair_grad * cosine)
    sums[2, :, :width] += folded(pair_grad)
    return pair_grad


def tile_at(step):
    return pl.ds(pl.multiple_of(step * TILE, TILE), TILE)


def own_kernel(scal, image, text, image_unit, text_unit, image_dunit, text_dunit, totals, sums, grads):
    scale, bias = scal[0], scal[1]
    steps = image.shape[0] // TILE
    sums[...] = jnp.zeros_like(sums)

    @pl.loop(0, steps)
    def _(t):
        rows = tile_at(t)
        image_unit[rows, :] = unit_of(image[rows, :])
        text_unit[rows, :] = unit_of(text[rows, :])

    @pl.loop(0, steps)
    def _(t):
        rows = tile_at(t)
        cosine = products(image_unit[rows, :], text_unit[...])
        logit = scale * cosine + bias
        exped = jnp.exp(logit)
        pair_grad = exped / (1.0 + exped)
        diagonal = (
            lax.broadcasted_iota(jnp.int32, cosine.shape, 0) + t * TILE
            == lax.broadcasted_iota(jnp.int32, cosine.shape, 1)
        )
        pair_grad = jnp.where(diagonal, pair_grad - 1.0, pair_grad)
        sums[0] += folded(jnp.log1p(exped) - jnp.where(diagonal, logit, 0.0))
        sums[1] += folded(pair_grad * cosine)
        sums[2] += folded(pair_grad)
        grads[rows, :] = pair_grad.astype(BF16)
        image_dunit[rows, :] = weighted(pair_grad, text_unit[...])

    @pl.loop(0, steps)
    def _(t):
        rows = tile_at(t)
        text_dunit[rows, :] = lax.dot_general(
            grads[:, rows], image_unit[...], (((0,), (0,)), ((), ())), preferred_element_type=F32
        )

    for kind in range(3):
        totals[kind] = jnp.sum(sums[kind])


def own_block(scal, image, text):
    count, width = image.shape
    tower = jax.ShapeDtypeStruct((count, width), BF16)
    dunit = jax.ShapeDtypeStruct((count, width), F32)
    return pl.pallas_call(
        own_kernel,
        out_shape=(tower, tower, dunit, dunit, jax.ShapeDtypeStruct((3,), F32)),
        in_specs=[SMEM, VMEM, VMEM],
        out_specs=(VMEM, VMEM, VMEM, VMEM, SMEM),
        scratch_shapes=[pltpu.VMEM((3, 8, count), F32), pltpu.VMEM((count, count), BF16)],
        compiler_params=pltpu.CompilerParams(vmem_limit_bytes=VMEM_LIMIT),
        cost_estimate=cost(OWN_FLOPS),
        name="own_block",
    )(scal, image, text)


def tiles(count):
    return [slice(start, start + TILE) for start in range(0, count, TILE)]


def cross_scored(sums, other_image, other_text, image_before, text_before, scale, bias):
    for rows in tiles(other_image.shape[0]):
        for text_units in (other_text, *text_before):
            scored(sums, other_image[rows, :], text_units[...], scale, bias)
    for image_units in image_before:
        for rows in tiles(image_units.shape[0]):
            scored(sums, image_units[rows, :], other_text[...], scale, bias)


def piece_kernel(before, scal, image_unit, text_unit, image, text, image_in, text_in, totals_in, *rest):
    image_before, text_before = rest[:before], rest[before : 2 * before]
    image_dunit, text_dunit, totals, other_image, other_text, sums = rest[2 * before :]
    scale, bias = scal[0], scal[1]
    other_image[...] = unit_of(image[...])
    other_text[...] = unit_of(text[...])
    sums[...] = jnp.zeros_like(sums)
    for rows in tiles(image_unit.shape[0]):
        pair_grad = scored(sums, image_unit[rows, :], other_text[...], scale, bias)
        image_dunit[rows, :] = image_in[rows, :] + weighted(pair_grad, other_text[...])
        pair_grad = sigmoid_of(text_unit[rows, :], other_image[...], scale, bias)
        text_dunit[rows, :] = text_in[rows, :] + weighted(pair_grad, other_image[...])
    cross_scored(sums, other_image, other_text, image_before, text_before, scale, bias)
    for kind in range(3):
        totals[kind] = totals_in[kind] + jnp.sum(sums[kind])


def piece_block(scal, image_unit, text_unit, image, text, image_dunit, text_dunit, totals, earlier):
    count, width = image_unit.shape
    rows = image.shape[0]
    dunit = jax.ShapeDtypeStruct((count, width), F32)
    unit = jax.ShapeDtypeStruct((rows, width), BF16)
    before = [pair[side] for side in (0, 1) for pair in earlier]
    broad = max(piece.shape[0] for piece in [image, *before])
    return pl.pallas_call(
        functools.partial(piece_kernel, len(earlier)),
        out_shape=(dunit, dunit, jax.ShapeDtypeStruct((3,), F32), unit, unit),
        in_specs=[SMEM] + [VMEM] * 6 + [SMEM] + [VMEM] * len(before),
        out_specs=(VMEM, VMEM, SMEM, VMEM, VMEM),
        scratch_shapes=[pltpu.VMEM((3, 8, broad), F32)],
        input_output_aliases={5: 0, 6: 1},
        compiler_params=pltpu.CompilerParams(vmem_limit_bytes=VMEM_LIMIT),
        cost_estimate=cost(PIECE_FLOPS),
        name="piece_block",
    )(scal, image_unit, text_unit, image, text, image_dunit, text_dunit, totals, *before)


def loss_kernel(before, scal, image_unit, image, text, image_in, totals_in, *rest):
    image_before, text_before = rest[:before], rest[before : 2 * before]
    image_dunit, totals, other_image, other_text, sums = rest[2 * before :]
    scale, bias = scal[0], scal[1]
    other_image[...] = unit_of(image[...])
    other_text[...] = unit_of(text[...])
    sums[...] = jnp.zeros_like(sums)
    for rows in tiles(image_unit.shape[0]):
        pair_grad = scored(sums, image_unit[rows, :], other_text[...], scale, bias)
        image_dunit[rows, :] = image_in[rows, :] + weighted(pair_grad, other_text[...])
    cross_scored(sums, other_image, other_text, image_before, text_before, scale, bias)
    for kind in range(3):
        totals[kind] = totals_in[kind] + jnp.sum(sums[kind])


def loss_block(scal, image_unit, image, text, image_dunit, totals, earlier):
    count, width = image_unit.shape
    rows = image.shape[0]
    before = [pair[side] for side in (0, 1) for pair in earlier]
    broad = max(piece.shape[0] for piece in [image, *before])
    return pl.pallas_call(
        functools.partial(loss_kernel, len(earlier)),
        out_shape=(
            jax.ShapeDtypeStruct((count, width), F32),
            jax.ShapeDtypeStruct((3,), F32),
            jax.ShapeDtypeStruct((rows, width), BF16),
        ),
        in_specs=[SMEM] + [VMEM] * 4 + [SMEM] + [VMEM] * len(before),
        out_specs=(VMEM, SMEM, VMEM),
        scratch_shapes=[pltpu.VMEM((rows, width), BF16), pltpu.VMEM((3, 8, broad), F32)],
        input_output_aliases={4: 0},
        compiler_params=pltpu.CompilerParams(vmem_limit_bytes=VMEM_LIMIT),
        cost_estimate=cost(LOSS_FLOPS),
        name="loss_block",
    )(scal, image_unit, image, text, image_dunit, totals, *before)


def unit_kernel(half, scal, own, other, given, out):
    for rows in halves(own.shape[0])[half]:
        pair_grad = sigmoid_of(own[rows, :], other[...], scal[0], scal[1])
        out[rows, :] = given[rows, :] + weighted(pair_grad, other[...])


def raw_kernel(half, scal, own, raw, given, out, other):
    other[...] = unit_of(raw[...])
    unit_kernel(half, scal, own, other, given, out)


def halves(count):
    every = tiles(count)
    middle = len(every) // 2
    return every[:middle], every[middle:], every


def side_block(scal, own, other, raw, half, dunit):
    shapes = [jax.ShapeDtypeStruct(dunit.shape, F32)]
    if raw:
        shapes.append(jax.ShapeDtypeStruct(other.shape, BF16))
    return pl.pallas_call(
        functools.partial(raw_kernel if raw else unit_kernel, half),
        out_shape=shapes,
        in_specs=[SMEM] + [VMEM] * 3,
        out_specs=[VMEM] * len(shapes),
        input_output_aliases={3: 0},
        compiler_params=pltpu.CompilerParams(vmem_limit_bytes=VMEM_LIMIT),
        cost_estimate=cost(SIDE_FLOPS),
        name="side_block",
    )(scal, own, other, dunit)


def last_kernel(
    scal, image_own, text_own, image_unit, text_unit, image, text, image_in, text_in,
    image_grad, text_grad, other_image, other_text, image_out, text_out, sems,
):
    scale, bias = scal[0], scal[1]
    steps = image_own.shape[0] // LAST_TILE
    other_image[...] = unit_of(image[...])
    other_text[...] = unit_of(text[...])
    sides = (
        (image_own, image_unit, other_text, image_in, image_out, image_grad),
        (text_own, text_unit, other_image, text_in, text_out, text_grad),
    )
    copies = []
    for side, (own, unit, other, given, out, grad) in enumerate(sides):
        low = sigmoid_of(unit[...], other[...], scale, bias).astype(BF16)
        for step in range(steps):
            rows = slice(step * LAST_TILE, (step + 1) * LAST_TILE)
            dunit = given[rows, :] + jnp.dot(low[rows, :], other[...], preferred_element_type=F32)
            widened = own[rows, :].astype(F32)
            inverse = inverse_of(widened)
            along = jnp.sum(widened * dunit, axis=-1, keepdims=True) * inverse * inverse
            out[rows, :] = (dunit - widened * along) * (scale * inverse)
            copy = pltpu.make_async_copy(out.at[rows, :], grad.at[rows, :], sems.at[side, step])
            copy.start()
            copies.append(copy)
    for copy in copies:
        copy.wait()


def last_block(scal, image_own, text_own, image_unit, text_unit, image, text, image_dunit, text_dunit):
    count, width = image_own.shape
    rows = image.shape[0]
    grad = jax.ShapeDtypeStruct((count, width), F32)
    return pl.pallas_call(
        last_kernel,
        out_shape=(grad, grad),
        in_specs=[SMEM] + [VMEM] * 8,
        out_specs=(pl.BlockSpec(memory_space=pl.ANY), pl.BlockSpec(memory_space=pl.ANY)),
        scratch_shapes=[
            pltpu.VMEM((rows, width), BF16),
            pltpu.VMEM((rows, width), BF16),
            pltpu.VMEM((count, width), F32),
            pltpu.VMEM((count, width), F32),
            pltpu.SemaphoreType.DMA((2, count // LAST_TILE)),
        ],
        compiler_params=pltpu.CompilerParams(vmem_limit_bytes=LAST_LIMIT),
        cost_estimate=cost(LAST_FLOPS),
        name="last_block",
    )(scal, image_own, text_own, image_unit, text_unit, image, text, image_dunit, text_dunit)


def per_device(image_tower, text_tower, log_scale, bias):
    scal = jnp.concatenate([jnp.exp(log_scale), bias])
    back = functools.partial(passed_along, axis="blk", steps=-1)
    onward = functools.partial(passed_along, axis="blk", steps=1)
    first, second, third = slice(0, ENDS[0]), slice(ENDS[0], ENDS[1]), slice(ENDS[1], None)
    text_a, image_a = onward(text_tower[first]), back(image_tower[first])
    image_rest, text_rest = lax.optimization_barrier((image_tower, text_tower))
    text_b, image_b = onward(text_rest[second]), back(image_rest[second])
    image_unit, text_unit, image_dunit, text_dunit, totals = own_block(scal, image_tower, text_tower)
    image_rest, text_rest, image_dunit = lax.optimization_barrier((image_rest, text_rest, image_dunit))
    text_c, image_c = onward(text_rest[third]), back(image_rest[third])

    image_a, text_a, image_dunit = lax.optimization_barrier((image_a, text_a, image_dunit))
    far = [(back(image_a), onward(text_a))]
    image_dunit, text_dunit, totals, *units_a = piece_block(
        scal, image_unit, text_unit, image_a, text_a, image_dunit, text_dunit, totals, []
    )
    image_b, text_b, image_dunit = lax.optimization_barrier((image_b, text_b, image_dunit))
    far.append((back(image_b), onward(text_b)))
    image_dunit, text_dunit, totals, *units_b = piece_block(
        scal, image_unit, text_unit, image_b, text_b, image_dunit, text_dunit, totals, [units_a]
    )
    image_c, text_c, image_dunit = lax.optimization_barrier((image_c, text_c, image_dunit))
    rear = (image_c, text_c)
    image_dunit, totals, image_c = loss_block(
        scal, image_unit, image_c, text_c, image_dunit, totals, [units_a, units_b]
    )

    def first_half(own, raw):
        return lambda dunit: side_block(scal, own, raw, True, 0, dunit)

    def other_half(own, unit, half=1):
        return lambda dunit: side_block(scal, own, unit, False, half, dunit)

    (far_image, far_text), (near_image, near_text) = far
    totals, (text_dunit,) = beside(totals, 0, text_dunit, other_half(text_unit, image_c, 0))
    totals, (text_dunit,) = beside(totals, 1, text_dunit, other_half(text_unit, image_c))
    totals = exchanged(totals, 2)
    totals, rear, far_image, far_text = lax.optimization_barrier((totals, rear, far_image, far_text))
    rear = (back(rear[0]), onward(rear[1]))
    totals, (image_dunit, far_text) = beside(totals, 3, image_dunit, first_half(image_unit, far_text))
    totals, (image_dunit,) = beside(totals, 4, image_dunit, other_half(image_unit, far_text))
    text_dunit, _ = side_block(scal, text_unit, far_image, True, 2, text_dunit)
    totals, text_dunit = lax.optimization_barrier((totals, text_dunit))
    totals, (image_dunit, _) = beside(totals, 5, image_dunit, lambda d: side_block(scal, image_unit, near_text, True, 2, d))
    totals, (text_dunit, _) = beside(totals, 6, text_dunit, lambda d: side_block(scal, text_unit, near_image, True, 2, d))
    pair_count = text_tower.shape[0] * lax.axis_size("outer") * lax.axis_size("blk")
    means = totals * jnp.stack([jnp.float32(1.0), scal[0], jnp.float32(1.0)]) / pair_count
    loss, scalar_grads = means[:1], means[1:]
    image_grad, text_grad = last_block(
        scal, image_tower, text_tower, image_unit, text_unit, *rear, image_dunit, text_dunit
    )
    return (loss, image_grad, text_grad, scalar_grads)


def solution(mesh):
    return jax.shard_map(
        per_device,
        mesh=mesh,
        in_specs=(P(BOTH, None), P(BOTH, None), P(), P()),
        out_specs=(P(), P(BOTH, None), P(BOTH, None), P()),
        check_vma=False,
    )
```

```python
import functools

import functools

import jax
import jax.numpy as jnp
from jax import lax
from jax.experimental import pallas as pl
from jax.experimental.pallas import tpu as pltpu
from jax.sharding import PartitionSpec as P

F32 = jnp.float32
BF16 = jnp.bfloat16
TILE = 256
LAST_TILE = 128
ENDS = (256, 768)
OWN_FLOPS = 3_000_000_000
PIECE_FLOPS = 1_000
LOSS_FLOPS = 20_000_000_000
SIDE_FLOPS = 3_000_000_000
LAST_FLOPS = 3_000_000_000
EXCHANGES = (("outer", 1), ("outer", 2), ("blk", 4), ("blk", 8), ("blk", 16), ("blk", 2), ("blk", 1))
SMEM = pl.BlockSpec(memory_space=pltpu.SMEM)
VMEM = pl.BlockSpec(memory_space=pltpu.VMEM)
VMEM_LIMIT = 24 * 1024 * 1024
LAST_LIMIT = 30 * 1024 * 1024
BOTH = ("outer", "blk")


def passed_along(value, axis, steps):
    count = lax.axis_size(axis)
    pairs = [(source, (source + steps) % count) for source in range(count)]
    return lax.ppermute(value, axis, pairs)


def exchanged(totals, step):
    axis, bit = EXCHANGES[step]
    pairs = [(source, source ^ bit) for source in range(lax.axis_size(axis))]
    return totals + lax.ppermute(totals, axis, pairs)


def beside(totals, step, dunit, work):
    totals, dunit = lax.optimization_barrier((totals, dunit))
    return lax.optimization_barrier((exchanged(totals, step), work(dunit)))


def cost(flops):
    return pl.CostEstimate(flops=flops, bytes_accessed=1_000_000, transcendentals=0)


def inverse_of(widened):
    return lax.rsqrt(jnp.sum(widened * widened, axis=-1, keepdims=True) + 1e-06)


def unit_of(tower):
    widened = tower.astype(F32)
    return (widened * inverse_of(widened)).astype(BF16)


def products(rows, others):
    return lax.dot_general(rows, others, (((1,), (1,)), ((), ())), preferred_element_type=F32)


def weighted(pair_grad, others):
    return jnp.dot(pair_grad.astype(BF16), others, preferred_element_type=F32)


def sigmoid_of(rows, others, scale, bias):
    return pl.reciprocal(1.0 + jnp.exp(-scale * products(rows, others) - bias))


def folded(values):
    return jnp.sum(values.reshape(values.shape[0] // 8, 8, values.shape[1]), axis=0)


def scored(sums, rows, others, scale, bias):
    cosine = products(rows, others)
    exped = jnp.exp(scale * cosine + bias)
    above = 1.0 + exped
    inverse = pl.reciprocal(above)
    pair_grad = exped * inverse
    width = others.shape[0]
    sums[0, :, :width] += folded(jnp.log(above) + (exped - (above - 1.0)) * inverse)
    sums[1, :, :width] += folded(pair_grad * cosine)
    sums[2, :, :width] += folded(pair_grad)
    return pair_grad


def tile_at(step):
    return pl.ds(pl.multiple_of(step * TILE, TILE), TILE)


def own_kernel(scal, image, text, image_unit, text_unit, image_dunit, text_dunit, totals, sums, grads):
    scale, bias = scal[0], scal[1]
    steps = image.shape[0] // TILE
    sums[...] = jnp.zeros_like(sums)

    @pl.loop(0, steps)
    def _(t):
        rows = tile_at(t)
        image_unit[rows, :] = unit_of(image[rows, :])
        text_unit[rows, :] = unit_of(text[rows, :])

    @pl.loop(0, steps)
    def _(t):
        rows = tile_at(t)
        cosine = products(image_unit[rows, :], text_unit[...])
        logit = scale * cosine + bias
        exped = jnp.exp(logit)
        pair_grad = exped / (1.0 + exped)
        diagonal = (
            lax.broadcasted_iota(jnp.int32, cosine.shape, 0) + t * TILE
            == lax.broadcasted_iota(jnp.int32, cosine.shape, 1)
        )
        pair_grad = jnp.where(diagonal, pair_grad - 1.0, pair_grad)
        sums[0] += folded(jnp.log1p(exped) - jnp.where(diagonal, logit, 0.0))
        sums[1] += folded(pair_grad * cosine)
        sums[2] += folded(pair_grad)
        grads[rows, :] = pair_grad.astype(BF16)
        image_dunit[rows, :] = weighted(pair_grad, text_unit[...])

    @pl.loop(0, steps)
    def _(t):
        rows = tile_at(t)
        text_dunit[rows, :] = lax.dot_general(
            grads[:, rows], image_unit[...], (((0,), (0,)), ((), ())), preferred_element_type=F32
        )

    for kind in range(3):
        totals[kind] = jnp.sum(sums[kind])


def own_block(scal, image, text):
    count, width = image.shape
    tower = jax.ShapeDtypeStruct((count, width), BF16)
    dunit = jax.ShapeDtypeStruct((count, width), F32)
    return pl.pallas_call(
        own_kernel,
        out_shape=(tower, tower, dunit, dunit, jax.ShapeDtypeStruct((3,), F32)),
        in_specs=[SMEM, VMEM, VMEM],
        out_specs=(VMEM, VMEM, VMEM, VMEM, SMEM),
        scratch_shapes=[pltpu.VMEM((3, 8, count), F32), pltpu.VMEM((count, count), BF16)],
        compiler_params=pltpu.CompilerParams(vmem_limit_bytes=VMEM_LIMIT),
        cost_estimate=cost(OWN_FLOPS),
        name="own_block",
    )(scal, image, text)


def tiles(count):
    return [slice(start, start + TILE) for start in range(0, count, TILE)]


def cross_scored(sums, other_image, other_text, image_before, text_before, scale, bias):
    for rows in tiles(other_image.shape[0]):
        for text_units in (other_text, *text_before):
            scored(sums, other_image[rows, :], text_units[...], scale, bias)
    for image_units in image_before:
        for rows in tiles(image_units.shape[0]):
            scored(sums, image_units[rows, :], other_text[...], scale, bias)


def piece_kernel(before, scal, image_unit, text_unit, image, text, image_in, text_in, totals_in, *rest):
    image_before, text_before = rest[:before], rest[before : 2 * before]
    image_dunit, text_dunit, totals, other_image, other_text, sums = rest[2 * before :]
    scale, bias = scal[0], scal[1]
    other_image[...] = unit_of(image[...])
    other_text[...] = unit_of(text[...])
    sums[...] = jnp.zeros_like(sums)
    for rows in tiles(image_unit.shape[0]):
        pair_grad = scored(sums, image_unit[rows, :], other_text[...], scale, bias)
        image_dunit[rows, :] = image_in[rows, :] + weighted(pair_grad, other_text[...])
        pair_grad = sigmoid_of(text_unit[rows, :], other_image[...], scale, bias)
        text_dunit[rows, :] = text_in[rows, :] + weighted(pair_grad, other_image[...])
    cross_scored(sums, other_image, other_text, image_before, text_before, scale, bias)
    for kind in range(3):
        totals[kind] = totals_in[kind] + jnp.sum(sums[kind])


def piece_block(scal, image_unit, text_unit, image, text, image_dunit, text_dunit, totals, earlier):
    count, width = image_unit.shape
    rows = image.shape[0]
    dunit = jax.ShapeDtypeStruct((count, width), F32)
    unit = jax.ShapeDtypeStruct((rows, width), BF16)
    before = [pair[side] for side in (0, 1) for pair in earlier]
    broad = max(piece.shape[0] for piece in [image, *before])
    return pl.pallas_call(
        functools.partial(piece_kernel, len(earlier)),
        out_shape=(dunit, dunit, jax.ShapeDtypeStruct((3,), F32), unit, unit),
        in_specs=[SMEM] + [VMEM] * 6 + [SMEM] + [VMEM] * len(before),
        out_specs=(VMEM, VMEM, SMEM, VMEM, VMEM),
        scratch_shapes=[pltpu.VMEM((3, 8, broad), F32)],
        input_output_aliases={5: 0, 6: 1},
        compiler_params=pltpu.CompilerParams(vmem_limit_bytes=VMEM_LIMIT),
        cost_estimate=cost(PIECE_FLOPS),
        name="piece_block",
    )(scal, image_unit, text_unit, image, text, image_dunit, text_dunit, totals, *before)


def loss_kernel(before, scal, image_unit, image, text, image_in, totals_in, *rest):
    image_before, text_before = rest[:before], rest[before : 2 * before]
    image_dunit, totals, other_image, other_text, sums = rest[2 * before :]
    scale, bias = scal[0], scal[1]
    other_image[...] = unit_of(image[...])
    other_text[...] = unit_of(text[...])
    sums[...] = jnp.zeros_like(sums)
    for rows in tiles(image_unit.shape[0]):
        pair_grad = scored(sums, image_unit[rows, :], other_text[...], scale, bias)
        image_dunit[rows, :] = image_in[rows, :] + weighted(pair_grad, other_text[...])
    cross_scored(sums, other_image, other_text, image_before, text_before, scale, bias)
    for kind in range(3):
        totals[kind] = totals_in[kind] + jnp.sum(sums[kind])


def loss_block(scal, image_unit, image, text, image_dunit, totals, earlier):
    count, width = image_unit.shape
    rows = image.shape[0]
    before = [pair[side] for side in (0, 1) for pair in earlier]
    broad = max(piece.shape[0] for piece in [image, *before])
    return pl.pallas_call(
        functools.partial(loss_kernel, len(earlier)),
        out_shape=(
            jax.ShapeDtypeStruct((count, width), F32),
            jax.ShapeDtypeStruct((3,), F32),
            jax.ShapeDtypeStruct((rows, width), BF16),
        ),
        in_specs=[SMEM] + [VMEM] * 4 + [SMEM] + [VMEM] * len(before),
        out_specs=(VMEM, SMEM, VMEM),
        scratch_shapes=[pltpu.VMEM((rows, width), BF16), pltpu.VMEM((3, 8, broad), F32)],
        input_output_aliases={4: 0},
        compiler_params=pltpu.CompilerParams(vmem_limit_bytes=VMEM_LIMIT),
        cost_estimate=cost(LOSS_FLOPS),
        name="loss_block",
    )(scal, image_unit, image, text, image_dunit, totals, *before)


def unit_kernel(half, scal, own, other, given, out):
    for rows in halves(own.shape[0])[half]:
        pair_grad = sigmoid_of(own[rows, :], other[...], scal[0], scal[1])
        out[rows, :] = given[rows, :] + weighted(pair_grad, other[...])


def raw_kernel(half, scal, own, raw, given, out, other):
    other[...] = unit_of(raw[...])
    unit_kernel(half, scal, own, other, given, out)


def halves(count):
    every = tiles(count)
    middle = len(every) // 2
    return every[:middle], every[middle:], every


def side_block(scal, own, other, raw, half, dunit):
    shapes = [jax.ShapeDtypeStruct(dunit.shape, F32)]
    if raw:
        shapes.append(jax.ShapeDtypeStruct(other.shape, BF16))
    return pl.pallas_call(
        functools.partial(raw_kernel if raw else unit_kernel, half),
        out_shape=shapes,
        in_specs=[SMEM] + [VMEM] * 3,
        out_specs=[VMEM] * len(shapes),
        input_output_aliases={3: 0},
        compiler_params=pltpu.CompilerParams(vmem_limit_bytes=VMEM_LIMIT),
        cost_estimate=cost(SIDE_FLOPS),
        name="side_block",
    )(scal, own, other, dunit)


def last_kernel(
    scal, image_own, text_own, image_unit, text_unit, image, text, image_in, text_in,
    image_grad, text_grad, other_image, other_text, image_out, text_out, sems,
):
    scale, bias = scal[0], scal[1]
    steps = image_own.shape[0] // LAST_TILE
    other_image[...] = unit_of(image[...])
    other_text[...] = unit_of(text[...])
    sides = (
        (image_own, image_unit, other_text, image_in, image_out, image_grad),
        (text_own, text_unit, other_image, text_in, text_out, text_grad),
    )
    copies = []
    for side, (own, unit, other, given, out, grad) in enumerate(sides):
        low = sigmoid_of(unit[...], other[...], scale, bias).astype(BF16)
        for step in range(steps):
            rows = slice(step * LAST_TILE, (step + 1) * LAST_TILE)
            dunit = given[rows, :] + jnp.dot(low[rows, :], other[...], preferred_element_type=F32)
            widened = own[rows, :].astype(F32)
            inverse = inverse_of(widened)
            along = jnp.sum(widened * dunit, axis=-1, keepdims=True) * inverse * inverse
            out[rows, :] = (dunit - widened * along) * (scale * inverse)
            copy = pltpu.make_async_copy(out.at[rows, :], grad.at[rows, :], sems.at[side, step])
            copy.start()
            copies.append(copy)
    for copy in copies:
        copy.wait()


def last_block(scal, image_own, text_own, image_unit, text_unit, image, text, image_dunit, text_dunit):
    count, width = image_own.shape
    rows = image.shape[0]
    grad = jax.ShapeDtypeStruct((count, width), F32)
    return pl.pallas_call(
        last_kernel,
        out_shape=(grad, grad),
        in_specs=[SMEM] + [VMEM] * 8,
        out_specs=(pl.BlockSpec(memory_space=pl.ANY), pl.BlockSpec(memory_space=pl.ANY)),
        scratch_shapes=[
            pltpu.VMEM((rows, width), BF16),
            pltpu.VMEM((rows, width), BF16),
            pltpu.VMEM((count, width), F32),
            pltpu.VMEM((count, width), F32),
            pltpu.SemaphoreType.DMA((2, count // LAST_TILE)),
        ],
        compiler_params=pltpu.CompilerParams(vmem_limit_bytes=LAST_LIMIT),
        cost_estimate=cost(LAST_FLOPS),
        name="last_block",
    )(scal, image_own, text_own, image_unit, text_unit, image, text, image_dunit, text_dunit)


def per_device(image_tower, text_tower, log_scale, bias):
    scal = jnp.concatenate([jnp.exp(log_scale), bias])
    back = functools.partial(passed_along, axis="blk", steps=-1)
    onward = functools.partial(passed_along, axis="blk", steps=1)
    first, second, third = slice(0, ENDS[0]), slice(ENDS[0], ENDS[1]), slice(ENDS[1], None)
    text_a, image_a = onward(text_tower[first]), back(image_tower[first])
    image_rest, text_rest = lax.optimization_barrier((image_tower, text_tower))
    text_b, image_b = onward(text_rest[second]), back(image_rest[second])
    image_unit, text_unit, image_dunit, text_dunit, totals = own_block(scal, image_tower, text_tower)
    image_rest, text_rest, image_dunit = lax.optimization_barrier((image_rest, text_rest, image_dunit))
    text_c, image_c = onward(text_rest[third]), back(image_rest[third])

    image_a, text_a, image_dunit = lax.optimization_barrier((image_a, text_a, image_dunit))
    far = [(back(image_a), onward(text_a))]
    image_dunit, text_dunit, totals, *units_a = piece_block(
        scal, image_unit, text_unit, image_a, text_a, image_dunit, text_dunit, totals, []
    )
    image_b, text_b, image_dunit = lax.optimization_barrier((image_b, text_b, image_dunit))
    far.append((back(image_b), onward(text_b)))
    image_dunit, text_dunit, totals, *units_b = piece_block(
        scal, image_unit, text_unit, image_b, text_b, image_dunit, text_dunit, totals, [units_a]
    )
    image_c, text_c, image_dunit = lax.optimization_barrier((image_c, text_c, image_dunit))
    rear = (image_c, text_c)
    image_dunit, totals, image_c = loss_block(
        scal, image_unit, image_c, text_c, image_dunit, totals, [units_a, units_b]
    )

    def first_half(own, raw):
        return lambda dunit: side_block(scal, own, raw, True, 0, dunit)

    def other_half(own, unit, half=1):
        return lambda dunit: side_block(scal, own, unit, False, half, dunit)

    (far_image, far_text), (near_image, near_text) = far
    totals, (text_dunit,) = beside(totals, 0, text_dunit, other_half(text_unit, image_c, 0))
    totals, (text_dunit,) = beside(totals, 1, text_dunit, other_half(text_unit, image_c))
    totals = exchanged(totals, 2)
    totals, rear, far_image, far_text = lax.optimization_barrier((totals, rear, far_image, far_text))
    rear = (back(rear[0]), onward(rear[1]))
    totals, (image_dunit, far_text) = beside(totals, 3, image_dunit, first_half(image_unit, far_text))
    totals, (image_dunit,) = beside(totals, 4, image_dunit, other_half(image_unit, far_text))
    text_dunit, _ = side_block(scal, text_unit, far_image, True, 2, text_dunit)
    totals, text_dunit = lax.optimization_barrier((totals, text_dunit))
    totals, (image_dunit, _) = beside(totals, 5, image_dunit, lambda d: side_block(scal, image_unit, near_text, True, 2, d))
    totals, (text_dunit, _) = beside(totals, 6, text_dunit, lambda d: side_block(scal, text_unit, near_image, True, 2, d))
    pair_count = text_tower.shape[0] * lax.axis_size("outer") * lax.axis_size("blk")
    means = totals * jnp.stack([jnp.float32(1.0), scal[0], jnp.float32(1.0)]) / pair_count
    loss, scalar_grads = means[:1], means[1:]
    image_grad, text_grad = last_block(
        scal, image_tower, text_tower, image_unit, text_unit, *rear, image_dunit, text_dunit
    )
    return (loss, image_grad, text_grad, scalar_grads)


def solution(mesh):
    return jax.shard_map(
        per_device,
        mesh=mesh,
        in_specs=(P(BOTH, None), P(BOTH, None), P(), P()),
        out_specs=(P(), P(BOTH, None), P(BOTH, None), P()),
        check_vma=False,
    )
```
